512 devices in a mesh: seg: 64 (over y, z), kvh: 8 (over x, core).
Axes of the slice: x: 4, y: 8, z: 8, core: 2. Of those that a mesh axis runs over, the one named last changes fastest.
Arguments:
- queries: bfloat16 [16384, 5120], P('seg', 'kvh'), may hold values from -12 to 12
- key_rows: bfloat16 [16384, 1024], P('seg', 'kvh'), may hold values from -4 to 4
- value_rows: bfloat16 [16384, 1024], P('seg', 'kvh'), may hold values from -6 to 6
- grad_out: bfloat16 [16384, 5120], P('seg', 'kvh'), may hold values from -48 to 48
- w_key: bfloat16 [5120, 1024], P(None, 'kvh'), may hold values from -0.125 to 0.125
- w_value: bfloat16 [5120, 1024], P(None, 'kvh'), may hold values from -0.125 to 0.125
- trunk_len: int32 [64], replicated, may hold values from 64 to 128
- leaf_len: int32 [64, 64], replicated, may hold values from 1 to 2, as said below
- leaf_tree: int32 [64, 64], replicated, may hold values from 0 to 63, as said below
Outputs:
- grad_query: bfloat16 [16384, 5120], P('seg', 'kvh')
- grad_hidden: bfloat16 [16384, 5120], P('seg', 'kvh')
The draws below stay inside these ranges and needn't reach their ends.
Inputs may be any that keep to these rules, and one draw needn't show every extreme that they name: `leaf_tree`: each row lists every device once. `leaf_len`: the leaves whose parent is one device, drawn anew, have 2 live positions.
All inputs are finite; a program needn't handle non-finite values.
Results may differ from the reference program's by a relative error of at most 0.018.
Values may be sent and summed in bfloat16 or wider, within the bound.
No kernel may reach another device: no remote copies, remote signals or barrier semaphores. Data moves between devices by JAX's collectives and lax.ppermute only.
A program may use at most 128 MiB of HBM per device.

```python
import math
import jax
import jax.numpy as jnp
from jax import lax

D = 5120
HD = 128
GROUP = 5
KVH = 8
QH = 40
TRUNK = 128
LEAF = 2
NLEAF = 64
TOK_DEV = 256
TOKENS = 16384
N_SEG = 64


def forest_lists(base_key):
    pick_key, rank_key, order_key, length_key = jax.random.split(base_key, 4)
    popular = jax.random.randint(pick_key, (), 0, N_SEG)
    ranks = jax.vmap(lambda subkey: jax.random.permutation(subkey, N_SEG))(jax.random.split(rank_key, N_SEG))
    ranks = jnp.where(jnp.arange(N_SEG)[None, :] == popular, -1, ranks)
    chosen = jnp.argsort(ranks, axis=1)[:, :NLEAF]
    shuffle = jax.vmap(lambda subkey: jax.random.permutation(subkey, NLEAF))(jax.random.split(order_key, N_SEG))
    tree_lists = jnp.take_along_axis(chosen, shuffle, axis=1).astype(jnp.int32)
    lengths = jax.random.randint(length_key, (N_SEG, NLEAF), LEAF // 2, LEAF + 1)
    lengths = jnp.where(tree_lists == popular, LEAF, lengths).astype(jnp.int32)
    return (tree_lists, lengths)


def draw_key_rows(key, part):
    key = jax.random.fold_in(key, 3)
    value_key = jax.random.fold_in(key, 1)
    values = jnp.clip(jax.random.normal(value_key, (TOKENS, KVH * HD)), -4.0, 4.0)
    return values.astype(jnp.bfloat16)


def draw_queries(key, part):
    key = jax.random.fold_in(key, 5)
    value_key = jax.random.fold_in(key, 1)
    values = jnp.clip(jax.random.normal(value_key, (TOKENS, QH * HD)), -4.0, 4.0)
    return values.astype(jnp.bfloat16)


def draw_trunk_len(key, part):
    key = jax.random.fold_in(key, 9)
    value_key, pick_key = jax.random.split(key)
    values = jax.random.randint(value_key, (N_SEG,), TRUNK // 2, TRUNK + 1)
    chosen = jax.random.randint(pick_key, (), 0, N_SEG)
    return jnp.where(jnp.arange(N_SEG) == chosen, TRUNK, values).astype(jnp.int32)


def draw_leaf_tree(key, part):
    tree_lists, lengths = forest_lists(key)
    return tree_lists


def draw_leaf_len(key, part):
    tree_lists, lengths = forest_lists(key)
    return lengths


def levels(own_key, shape, pieces, low, top_value):
    loudness, own = 1.0, jax.random.fold_in(own_key, 6)
    for axis_at, shards_of in pieces:
        steps = jnp.exp(jax.random.uniform(jax.random.fold_in(own, axis_at), (shards_of,), jnp.float32, low / len(pieces), top_value / len(pieces)))
        loudness = loudness * jnp.repeat(steps, shape[axis_at] // shards_of).reshape([-1 if axis == axis_at else 1 for axis in range(len(shape))])
    return loudness


def normal_values(stream_key, extent, spread, limit, cuts=(), dtype=jnp.bfloat16):
    drawn = jax.random.normal(stream_key, extent, jnp.float32) * spread
    if len(cuts) > 0:
        drawn = levels(stream_key, extent, cuts, -0.22, 0.18) * drawn
    return jnp.clip(drawn, min=-limit, max=limit).astype(dtype)


def setup_inputs(seed: int = 0) -> dict:
    splits = jax.random.split(jax.random.key(seed), 10)
    queries = draw_queries(jax.random.fold_in(splits[9], 71), 0)
    key_rows = draw_key_rows(jax.random.fold_in(splits[9], 71), 0)
    value_rows = normal_values(splits[2], (TOKENS, KVH * HD), 1.0, 6.0, ((0, 64), (1, 8)))
    grad_out = normal_values(splits[3], (TOKENS, QH * HD), 8.0, 48.0, ((0, 64), (1, 8)))
    w_key = normal_values(splits[4], (D, KVH * HD), (2 * HD * KVH) ** -0.5, 0.125, ((1, 8),))
    w_value = normal_values(splits[5], (D, KVH * HD), (2 * HD * KVH) ** -0.5, 0.125, ((1, 8),))
    trunk_len = draw_trunk_len(jax.random.fold_in(splits[9], 71), 0)
    leaf_len = draw_leaf_len(jax.random.fold_in(splits[9], 71), 0)
    leaf_tree = draw_leaf_tree(jax.random.fold_in(splits[9], 71), 0)
    return dict(queries=queries, key_rows=key_rows, value_rows=value_rows, grad_out=grad_out, w_key=w_key, w_value=w_value, trunk_len=trunk_len, leaf_len=leaf_len, leaf_tree=leaf_tree)


very_negative = -1e+30

def pair_products(query_rows, key_cols):
    batch_size, row_count, row_width = query_rows.shape
    head_rows = query_rows.astype(jnp.float32).reshape(batch_size, row_count, GROUP, row_width // GROUP)
    return jnp.einsum('brgd,bcd->bgrc', head_rows, key_cols.astype(jnp.float32), precision=lax.Precision.HIGHEST)

def partial_stats(scores, prob_grad, visible):
    masked = visible[:, None]
    row_max = lax.optimization_barrier(jnp.max(jnp.where(masked, scores, very_negative), axis=-1))
    weights = jnp.where(masked, jnp.exp(scores - row_max[..., None]), 0.0)
    return (row_max, lax.optimization_barrier(jnp.sum(weights, axis=-1)), lax.optimization_barrier(jnp.sum(weights * prob_grad, axis=-1)))

def finish_stats(stats):
    row_total = jnp.maximum(stats[1], 1.0)
    return (stats[0] + jnp.log(row_total), stats[2] / row_total)

def row_grads(query_rows, grad_rows, key_cols, value_cols, visible, scores, prob_grad, log_total, row_delta):
    batch_size, row_count, row_width = query_rows.shape
    head_size = row_width // GROUP
    score_scale = 1.0 / math.sqrt(head_size)
    probability = jnp.where(visible[:, None], jnp.exp(scores - log_total[..., None]), 0.0)
    score_grad = (probability * (prob_grad - row_delta[..., None])).astype(jnp.bfloat16).astype(jnp.float32)
    probability_low = probability.astype(jnp.bfloat16).astype(jnp.float32)
    head_rows = query_rows.astype(jnp.float32).reshape(batch_size, row_count, GROUP, head_size)
    head_grads = grad_rows.astype(jnp.float32).reshape(batch_size, row_count, GROUP, head_size)
    highest = lax.Precision.HIGHEST
    query_grad = jnp.einsum('bgrc,bcd->brgd', score_grad, key_cols.astype(jnp.float32), precision=highest) * score_scale
    key_grad = jnp.einsum('bgrc,brgd->bcd', score_grad, head_rows, precision=highest) * score_scale
    value_grad = jnp.einsum('bgrc,brgd->bcd', probability_low, head_grads, precision=highest)
    return (query_grad.reshape(batch_size, row_count, row_width), key_grad, value_grad)

def block_grads(query_rows, grad_rows, key_cols, value_cols, visible):
    score_scale = 1.0 / math.sqrt(key_cols.shape[-1])
    scores = pair_products(query_rows, key_cols) * score_scale
    prob_grad = pair_products(grad_rows, value_cols)
    log_total, row_delta = finish_stats(partial_stats(scores, prob_grad, visible))
    return row_grads(query_rows, grad_rows, key_cols, value_cols, visible, scores, prob_grad, log_total, row_delta)

def reference(queries, key_rows, value_rows, grad_out, w_key, w_value, trunk_len, leaf_len, leaf_tree):
    row_width = GROUP * HD

    def by_device(values, columns):
        return values.reshape(N_SEG, TOK_DEV, KVH, columns).transpose(0, 2, 1, 3)
    query_dev = by_device(queries, row_width)
    grad_dev = by_device(grad_out, row_width)
    key_dev = by_device(key_rows, HD)
    value_dev = by_device(value_rows, HD)
    positions = jnp.arange(TRUNK)
    leaf_pos = jnp.arange(LEAF)

    def trunk_step(device):
        visible = (positions[None, :] <= positions[:, None]) & (positions[:, None] < trunk_len[device])
        visible = jnp.broadcast_to(visible, (KVH, TRUNK, TRUNK))
        return block_grads(query_dev[device][:, :TRUNK], grad_dev[device][:, :TRUNK], key_dev[device][:, :TRUNK], value_dev[device][:, :TRUNK], visible)
    trunk_dq, trunk_dk, trunk_dv = lax.map(trunk_step, jnp.arange(N_SEG))

    def leaf_step(accumulated, device):
        key_sums, value_sums = accumulated
        tree_row = leaf_tree[device]
        lengths = leaf_len[device]

        def one_leaf(leaf_index):
            row_start = (TRUNK + leaf_index * LEAF).astype(jnp.int32)
            tree_index = tree_row[leaf_index]

            def rows_of(values):
                return lax.dynamic_slice_in_dim(values[device], row_start, LEAF, axis=1)
            key_cols = jnp.concatenate([key_dev[tree_index][:, :TRUNK], rows_of(key_dev)], axis=1)
            value_cols = jnp.concatenate([value_dev[tree_index][:, :TRUNK], rows_of(value_dev)], axis=1)
            trunk_part = (positions[None, :] < trunk_len[tree_index]) & (leaf_pos[:, None] < lengths[leaf_index])
            own_part = (leaf_pos[None, :] <= leaf_pos[:, None]) & (leaf_pos[:, None] < lengths[leaf_index])
            visible = jnp.broadcast_to(jnp.concatenate([trunk_part, own_part], axis=1), (KVH, LEAF, TRUNK + LEAF))
            return block_grads(rows_of(query_dev), rows_of(grad_dev), key_cols, value_cols, visible)
        leaf_dq, cols_dk, cols_dv = jax.vmap(one_leaf)(jnp.arange(NLEAF))
        key_sums = key_sums.at[tree_row].add(cols_dk[:, :, :TRUNK])
        value_sums = value_sums.at[tree_row].add(cols_dv[:, :, :TRUNK])
        return ((key_sums, value_sums), (leaf_dq, cols_dk[:, :, TRUNK:], cols_dv[:, :, TRUNK:]))
    empty_sums = jnp.zeros((N_SEG, KVH, TRUNK, HD), jnp.float32)
    sums_out, leaf_out = lax.scan(leaf_step, (empty_sums, empty_sums), jnp.arange(N_SEG))
    key_sums, value_sums = sums_out
    leaf_dq, leaf_dk, leaf_dv = leaf_out

    def leaf_layout(values):
        moved = values.transpose(0, 2, 1, 3, 4)
        return moved.reshape(N_SEG, KVH, NLEAF * LEAF, values.shape[-1])
    all_dq = jnp.concatenate([trunk_dq, leaf_layout(leaf_dq)], axis=2)
    grad_query = all_dq.transpose(0, 2, 1, 3).reshape(TOKENS, QH * HD).astype(jnp.bfloat16)
    key_grad = jnp.concatenate([trunk_dk + key_sums, leaf_layout(leaf_dk)], axis=2).astype(jnp.bfloat16)
    value_grad = jnp.concatenate([trunk_dv + value_sums, leaf_layout(leaf_dv)], axis=2).astype(jnp.bfloat16)
    weight_k = w_key.reshape(D, KVH, HD).astype(jnp.float32)
    weight_v = w_value.reshape(D, KVH, HD).astype(jnp.float32)

    def hidden_step(device):
        highest = lax.Precision.HIGHEST
        head_part = jnp.einsum('hrd,chd->hrc', key_grad[device].astype(jnp.float32), weight_k, precision=highest)
        head_part = head_part + jnp.einsum('hrd,chd->hrc', value_grad[device].astype(jnp.float32), weight_v, precision=highest)
        head_part = lax.optimization_barrier(head_part.astype(jnp.bfloat16)).astype(jnp.float32)
        return lax.optimization_barrier(jnp.sum(head_part, axis=0)).astype(jnp.bfloat16)
    grad_hidden = lax.map(hidden_step, jnp.arange(N_SEG)).reshape(TOKENS, D)
    return (grad_query, grad_hidden)
```

```python
import functools
import math

import jax
import jax.numpy as jnp
from jax import lax
from jax.experimental import pallas as pl
from jax.experimental.pallas import tpu as pltpu
from jax.sharding import PartitionSpec as P

GROUP = 5
TRUNK = 128
LEAF = 2
HEAD = 128
OUT_TILES = 2 * GROUP + 2
OUT_ROWS = OUT_TILES * LEAF
BACK_TILES = GROUP + 2
BACK_ROWS = 16
VERY_NEGATIVE = -1e30
SCALE = 1.0 / math.sqrt(HEAD)

f32 = jnp.float32
bf16 = jnp.bfloat16
vmem = pl.BlockSpec(memory_space=pltpu.VMEM)
smem = pl.BlockSpec(memory_space=pltpu.SMEM)


def dot(a, b, contract):
    return lax.dot_general(a, b, ((contract[0:1], contract[1:2]), ((), ())), preferred_element_type=f32)


def leaf_selector(leaf_tree_ref, seg):
    count = leaf_tree_ref.shape[0]
    tree_row = leaf_tree_ref[pl.ds(seg, 1), :].astype(f32).astype(bf16)
    tree_rows = jnp.broadcast_to(tree_row, (16, count))
    leaf = lax.broadcasted_iota(jnp.int32, (count, LEAF * count), 0)
    col = lax.broadcasted_iota(jnp.int32, (count, LEAF * count), 1)
    repeat = (leaf == (col >> 1)).astype(f32).astype(bf16)
    tree_of_col = dot(tree_rows, repeat, (1, 0))[0:1, :].astype(jnp.int32)
    row = lax.broadcasted_iota(jnp.int32, (LEAF * count, LEAF * count), 0)
    col = lax.broadcasted_iota(jnp.int32, (LEAF * count, LEAF * count), 1)
    row_pos = (row >= count).astype(jnp.int32)
    hit = (tree_of_col == row - row_pos * count) & (row_pos == (col & 1))
    return hit.astype(f32).astype(bf16)


def send_kernel(q_ref, g_ref, k_ref, v_ref, leaf_tree_ref, out_ref, rows_ref):
    count = leaf_tree_ref.shape[0]
    seg = lax.axis_index("seg")
    selector = leaf_selector(leaf_tree_ref, seg)
    leaf_rows = LEAF * count
    tile = 0
    for ref in (q_ref, g_ref, k_ref, v_ref):
        moved = dot(selector, ref[TRUNK : TRUNK + leaf_rows, :], (1, 0))
        for part in range(ref.shape[1] // HEAD):
            for a in range(LEAF):
                rows_ref[pl.ds(tile * LEAF + a, count, OUT_ROWS), :] = moved[
                    a * count : (a + 1) * count, part * HEAD : (part + 1) * HEAD
                ]
            tile += 1
    out_ref[...] = rows_ref[...].astype(bf16)


def softmax_grads(scores, prob_grad, visible):
    masked = jnp.where(visible, scores, VERY_NEGATIVE)
    row_max = jnp.max(masked, axis=-1, keepdims=True)
    weights = jnp.where(visible, jnp.exp(masked - row_max), 0.0)
    row_total = jnp.maximum(jnp.sum(weights, axis=-1, keepdims=True), 1.0)
    probability = weights * (1.0 / row_total)
    row_delta = jnp.sum(probability * prob_grad, axis=-1, keepdims=True)
    score_grad = (probability * (prob_grad - row_delta)).astype(bf16)
    return probability.astype(bf16), score_grad


def trunk_kernel(q_ref, g_ref, k_ref, v_ref, trunk_len_ref, dq_ref, dk_ref, dv_ref):
    seg = lax.axis_index("seg")
    trunk_len = trunk_len_ref[seg]
    keys = k_ref[0:TRUNK, :]
    values = v_ref[0:TRUNK, :]
    row = lax.broadcasted_iota(jnp.int32, (TRUNK, TRUNK), 0)
    col = lax.broadcasted_iota(jnp.int32, (TRUNK, TRUNK), 1)
    visible = (col <= row) & (row < trunk_len)
    for g in range(GROUP):
        head_q = q_ref[0:TRUNK, g * HEAD : (g + 1) * HEAD]
        head_g = g_ref[0:TRUNK, g * HEAD : (g + 1) * HEAD]
        scores = dot(head_q, keys, (1, 1)) * SCALE
        prob_grad = dot(head_g, values, (1, 1))
        probability, score_grad = softmax_grads(scores, prob_grad, visible)
        dq_ref[:, g * HEAD : (g + 1) * HEAD] = (dot(score_grad, keys, (1, 0)) * SCALE).astype(bf16)
        head_dk = dot(score_grad, head_q, (0, 0))
        head_dv = dot(probability, head_g, (0, 0))
        if g == 0:
            dk_ref[...] = head_dk
            dv_ref[...] = head_dv
        else:
            dk_ref[...] += head_dk
            dv_ref[...] += head_dv


def leaf_kernel(
    in_ref, k_ref, v_ref, trunk_dk_ref, trunk_dv_ref, leaf_tree_ref, leaf_len_ref, trunk_len_ref,
    out_ref, trunk_kv_ref, rows_ref, back_ref, dk_ref, dv_ref,
):
    count = leaf_tree_ref.shape[0]
    seg = lax.axis_index("seg")
    trunk_len = trunk_len_ref[seg]
    rows_ref[...] = in_ref[...].astype(f32)

    def gather(tile):
        parts = [rows_ref[pl.ds(tile * LEAF + a, count, OUT_ROWS), :] for a in range(LEAF)]
        return jnp.concatenate(parts, axis=0).astype(bf16)

    keys = jnp.concatenate([k_ref[0:TRUNK, :], gather(2 * GROUP)], axis=0)
    values = jnp.concatenate([v_ref[0:TRUNK, :], gather(2 * GROUP + 1)], axis=0)
    in_len = jnp.sum(jnp.where(leaf_tree_ref[...] == seg, leaf_len_ref[...], 0), axis=1, keepdims=True)
    row_len = jnp.concatenate([in_len] * LEAF, axis=0)
    leaf_rows = LEAF * count
    shape = (leaf_rows, TRUNK + leaf_rows)
    row = lax.broadcasted_iota(jnp.int32, shape, 0)
    col = lax.broadcasted_iota(jnp.int32, shape, 1)
    row_pos = (row >= count).astype(jnp.int32)
    leaf_col = col - TRUNK
    col_pos = (leaf_col >= count).astype(jnp.int32)
    own = (row - row_pos * count == leaf_col - col_pos * count) & (col_pos <= row_pos)
    visible = ((col < trunk_len) & (col < TRUNK)) | ((col >= TRUNK) & own)
    visible = visible & (row_pos < row_len)
    for g in range(GROUP):
        head_q = gather(g)
        head_g = gather(GROUP + g)
        scores = dot(head_q, keys, (1, 1)) * SCALE
        prob_grad = dot(head_g, values, (1, 1))
        probability, score_grad = softmax_grads(scores, prob_grad, visible)
        head_dq = dot(score_grad, keys, (1, 0)) * SCALE
        for a in range(LEAF):
            back_ref[pl.ds(g * LEAF + a, count, BACK_ROWS), :] = head_dq[a * count : (a + 1) * count, :]
        head_dk = dot(score_grad, head_q, (0, 0))
        head_dv = dot(probability, head_g, (0, 0))
        if g == 0:
            dk_ref[...] = head_dk
            dv_ref[...] = head_dv
        else:
            dk_ref[...] += head_dk
            dv_ref[...] += head_dv
    for a in range(LEAF):
        at = TRUNK + a * count
        back_ref[pl.ds(GROUP * LEAF + a, count, BACK_ROWS), :] = dk_ref[at : at + count, :] * SCALE
        back_ref[pl.ds((GROUP + 1) * LEAF + a, count, BACK_ROWS), :] = dv_ref[at : at + count, :]
    for spare in range(BACK_TILES * LEAF, BACK_ROWS):
        back_ref[pl.ds(spare, count, BACK_ROWS), :] = jnp.zeros((count, HEAD), f32)
    out_ref[...] = back_ref[...].astype(bf16)
    trunk_kv_ref[:, 0:HEAD] = (trunk_dk_ref[...] + dk_ref[0:TRUNK, :]) * SCALE
    trunk_kv_ref[:, HEAD : 2 * HEAD] = trunk_dv_ref[...] + dv_ref[0:TRUNK, :]


def back_kernel(in_ref, trunk_dq_ref, leaf_tree_ref, dq_ref, leaf_kv_ref, rows_ref):
    count = leaf_tree_ref.shape[0]
    seg = lax.axis_index("seg")
    selector = leaf_selector(leaf_tree_ref, seg)
    rows_ref[...] = in_ref[...].astype(f32)
    leaf_rows = LEAF * count
    for tile in range(BACK_TILES):
        parts = [rows_ref[pl.ds(tile * LEAF + a, count, BACK_ROWS), :] for a in range(LEAF)]
        moved = dot(selector, jnp.concatenate(parts, axis=0).astype(bf16), (0, 0)).astype(bf16)
        if tile < GROUP:
            dq_ref[TRUNK : TRUNK + leaf_rows, tile * HEAD : (tile + 1) * HEAD] = moved
        else:
            at = (tile - GROUP) * HEAD
            leaf_kv_ref[:, at : at + HEAD] = moved
    dq_ref[0:TRUNK, :] = trunk_dq_ref[...]


def hidden_sum(kv_ref, kept_refs, swapped_ref):
    rows = kv_ref.shape[0] // (2 * len(kept_refs))
    kvh = lax.axis_index("kvh")
    chip, core = kvh >> 1, kvh & 1
    chips = len(kept_refs)
    total = None
    for step in range(chips):
        from_chip = lax.rem(chip + chips - step, chips)
        for other in range(2):
            head = 2 * from_chip + (core if other == 0 else 1 - core)
            kv = kv_ref[pl.ds(pl.multiple_of(head * rows, rows), rows), :].astype(bf16)
            for part in range(2):
                if other == 0:
                    weight = kept_refs[step][part, core]
                else:
                    weight = swapped_ref[step, part]
                term = dot(kv[:, part * HEAD : (part + 1) * HEAD], weight, (1, 1))
                total = term if total is None else total + term
    return total.astype(bf16)


def hidden_trunk_kernel(kv_ref, swapped_ref, *refs):
    refs[-1][...] = hidden_sum(kv_ref, refs[:-1], swapped_ref)


def hidden_leaf_kernel(kv_ref, trunk_ref, swapped_ref, *refs):
    out_ref = refs[-1]
    out_ref[0:TRUNK, :] = trunk_ref[...]
    out_ref[TRUNK:, :] = hidden_sum(kv_ref, refs[:-1], swapped_ref)


def call(kernel, outs, in_specs, scratch=(), flops=0, moved=0):
    many = isinstance(outs, list)
    return pl.pallas_call(
        kernel,
        out_shape=outs,
        in_specs=in_specs,
        out_specs=[vmem] * len(outs) if many else vmem,
        scratch_shapes=list(scratch),
        compiler_params=pltpu.CompilerParams(vmem_limit_bytes=48 * 1024 * 1024),
        cost_estimate=pl.CostEstimate(flops=flops, bytes_accessed=moved, transcendentals=0),
    )


def shards(queries, key_rows, value_rows, grad_out, w_key, w_value, trunk_len, leaf_len, leaf_tree):
    count = lax.axis_size("seg")
    heads = lax.axis_size("kvh")
    chips = heads // 2
    leaf_rows = LEAF * count
    row_width = queries.shape[1]
    hidden = w_key.shape[0]
    kvh = lax.axis_index("kvh")
    chip, core = kvh // 2, kvh % 2
    out = jax.ShapeDtypeStruct

    send = call(
        send_kernel,
        out((count * OUT_ROWS, HEAD), bf16),
        [vmem] * 5,
        [pltpu.VMEM((count * OUT_ROWS, HEAD), f32)],
        flops=10**8,
        moved=10**6,
    )(queries, grad_out, key_rows, value_rows, leaf_tree)
    got = lax.all_to_all(
        send.reshape(count, OUT_ROWS, HEAD), "seg", split_axis=0, concat_axis=0, tiled=True
    ).reshape(count * OUT_ROWS, HEAD)

    per_chip = hidden // chips

    def piece(step):
        at = lax.rem(chip + step, chips) * per_chip
        parts = [lax.dynamic_slice_in_dim(w, at, per_chip, axis=0) for w in (w_key, w_value)]
        return jnp.stack(parts).reshape(2, 2, per_chip // 2, HEAD)

    kept = [piece(0)]
    for step in range(1, chips):
        route = [(2 * x + c, 2 * ((x + step) % chips) + c) for x in range(chips) for c in range(2)]
        kept.append(lax.ppermute(piece(step), "kvh", route))
    for_other = jnp.stack([lax.dynamic_index_in_dim(w, 1 - core, 1, keepdims=False) for w in kept])
    swapped = lax.ppermute(for_other, "kvh", [(i, i ^ 1) for i in range(heads)])

    trunk_dq, trunk_dk, trunk_dv = call(
        trunk_kernel,
        [out((TRUNK, row_width), bf16), out((TRUNK, HEAD), f32), out((TRUNK, HEAD), f32)],
        [vmem] * 4 + [smem],
        flops=5 * 2 * GROUP * TRUNK * TRUNK * HEAD,
        moved=10**6,
    )(queries, grad_out, key_rows, value_rows, trunk_len)

    keys_all = TRUNK + leaf_rows
    back, trunk_kv = call(
        leaf_kernel,
        [out((count * BACK_ROWS, HEAD), bf16), out((TRUNK, 2 * HEAD), f32)],
        [vmem] * 7 + [smem],
        [
            pltpu.VMEM((count * OUT_ROWS, HEAD), f32),
            pltpu.VMEM((count * BACK_ROWS, HEAD), f32),
            pltpu.VMEM((keys_all, HEAD), f32),
            pltpu.VMEM((keys_all, HEAD), f32),
        ],
        flops=5 * 2 * GROUP * leaf_rows * keys_all * HEAD,
        moved=10**6,
    )(got, key_rows, value_rows, trunk_dk, trunk_dv, leaf_tree, leaf_len, trunk_len)

    trunk_all = lax.all_gather(trunk_kv, "kvh", axis=0, tiled=True)
    back = lax.all_to_all(
        back.reshape(count, BACK_ROWS, HEAD), "seg", split_axis=0, concat_axis=0, tiled=True
    ).reshape(count * BACK_ROWS, HEAD)
    grad_query, leaf_kv = call(
        back_kernel,
        [out(queries.shape, bf16), out((leaf_rows, 2 * HEAD), bf16)],
        [vmem] * 3,
        [pltpu.VMEM((count * BACK_ROWS, HEAD), f32)],
        flops=10**8,
        moved=10**6,
    )(back, trunk_dq, leaf_tree)
    leaf_all = lax.all_gather(leaf_kv, "kvh", axis=0, tiled=True)
    columns = hidden // heads
    flops = 2 * TRUNK * 2 * HEAD * heads * columns
    hidden_trunk = call(
        hidden_trunk_kernel, out((TRUNK, columns), bf16), [vmem] * (2 + chips), flops=flops, moved=4 * 10**6
    )(trunk_all, swapped, *kept)
    grad_hidden = call(
        hidden_leaf_kernel, out((TRUNK + leaf_rows, columns), bf16), [vmem] * (3 + chips), flops=flops, moved=4 * 10**6
    )(leaf_all, hidden_trunk, swapped, *kept)
    return (grad_query, grad_hidden)


def solution(mesh):
    in_specs = (
        P("seg", "kvh"),
        P("seg", "kvh"),
        P("seg", "kvh"),
        P("seg", "kvh"),
        P(None, "kvh"),
        P(None, "kvh"),
        P(),
        P(),
        P(),
    )
    out_specs = (P("seg", "kvh"), P("seg", "kvh"))
    return jax.shard_map(shards, mesh=mesh, in_specs=in_specs, out_specs=out_specs, check_vma=False)
```

```python
import functools
import math

import jax
import jax.numpy as jnp
from jax import lax
from jax.experimental import pallas as pl
from jax.experimental.pallas import tpu as pltpu
from jax.sharding import PartitionSpec as P

GROUP = 5
TRUNK = 128
LEAF = 2
HEAD = 128
OUT_TILES = 2 * GROUP + 2
OUT_ROWS = OUT_TILES * LEAF
BACK_TILES = GROUP + 2
BACK_ROWS = 16
VERY_NEGATIVE = -1e30
SCALE = 1.0 / math.sqrt(HEAD)

f32 = jnp.float32
bf16 = jnp.bfloat16
vmem = pl.BlockSpec(memory_space=pltpu.VMEM)
smem = pl.BlockSpec(memory_space=pltpu.SMEM)
hbm = pl.BlockSpec(memory_space=pltpu.HBM)


def dot(a, b, contract):
    return lax.dot_general(a, b, ((contract[0:1], contract[1:2]), ((), ())), preferred_element_type=f32)


def leaf_selector(leaf_tree_ref, seg):
    count = leaf_tree_ref.shape[0]
    tree_row = leaf_tree_ref[pl.ds(seg, 1), :].astype(f32).astype(bf16)
    tree_rows = jnp.broadcast_to(tree_row, (16, count))
    leaf = lax.broadcasted_iota(jnp.int32, (count, LEAF * count), 0)
    col = lax.broadcasted_iota(jnp.int32, (count, LEAF * count), 1)
    repeat = (leaf == (col >> 1)).astype(f32).astype(bf16)
    tree_of_col = dot(tree_rows, repeat, (1, 0))[0:1, :].astype(jnp.int32)
    row = lax.broadcasted_iota(jnp.int32, (LEAF * count, LEAF * count), 0)
    col = lax.broadcasted_iota(jnp.int32, (LEAF * count, LEAF * count), 1)
    row_pos = (row >= count).astype(jnp.int32)
    hit = (tree_of_col == row - row_pos * count) & (row_pos == (col & 1))
    return hit.astype(f32).astype(bf16)


def copies(pairs, sems):
    started = [pltpu.make_async_copy(src, dst, sems.at[i]) for i, (src, dst) in enumerate(pairs)]
    for copy in started:
        copy.start()
    return started


def send_kernel(
    q_ref, g_ref, k_ref, v_ref, leaf_tree_ref,
    out_ref, tree_ref, q_buf, g_buf, k_buf, v_buf, rows_ref, out_buf, sems, out_sem,
):
    count = tree_ref.shape[0]
    leaves = pl.ds(TRUNK, LEAF * count)
    loads = [(leaf_tree_ref, tree_ref)]
    loads += [(src.at[leaves, :], dst) for src, dst in zip((q_ref, g_ref, k_ref, v_ref), (q_buf, g_buf, k_buf, v_buf))]
    loads = copies(loads, sems)
    seg = lax.axis_index("seg")
    loads[0].wait()
    selector = leaf_selector(tree_ref, seg)
    tile = 0
    for load, ref in zip(loads[1:], (q_buf, g_buf, k_buf, v_buf)):
        load.wait()
        moved = dot(selector, ref[...], (1, 0))
        for part in range(ref.shape[1] // HEAD):
            for a in range(LEAF):
                rows_ref[pl.ds(tile * LEAF + a, count, OUT_ROWS), :] = moved[
                    a * count : (a + 1) * count, part * HEAD : (part + 1) * HEAD
                ]
            tile += 1
    out_buf[...] = rows_ref[...].astype(bf16)
    store = pltpu.make_async_copy(out_buf, out_ref, out_sem)
    store.start()
    store.wait()


def softmax_grads(scores, prob_grad, visible):
    masked = jnp.where(visible, scores, VERY_NEGATIVE)
    row_max = jnp.max(masked, axis=-1, keepdims=True)
    weights = jnp.where(visible, jnp.exp(masked - row_max), 0.0)
    row_total = jnp.maximum(jnp.sum(weights, axis=-1, keepdims=True), 1.0)
    probability = weights * (1.0 / row_total)
    row_delta = jnp.sum(probability * prob_grad, axis=-1, keepdims=True)
    score_grad = (probability * (prob_grad - row_delta)).astype(bf16)
    return probability.astype(bf16), score_grad


def leaf_visible(leaf_tree_ref, leaf_len_ref, trunk_len, seg):
    count = leaf_tree_ref.shape[0]
    in_len = jnp.sum(jnp.where(leaf_tree_ref[...] == seg, leaf_len_ref[...], 0), axis=1, keepdims=True)
    row_len = jnp.concatenate([in_len] * LEAF, axis=0)
    leaf_rows = LEAF * count
    shape = (leaf_rows, TRUNK + leaf_rows)
    row = lax.broadcasted_iota(jnp.int32, shape, 0)
    col = lax.broadcasted_iota(jnp.int32, shape, 1)
    row_pos = (row >= count).astype(jnp.int32)
    leaf_col = col - TRUNK
    col_pos = (leaf_col >= count).astype(jnp.int32)
    own = (row - row_pos * count == leaf_col - col_pos * count) & (col_pos <= row_pos)
    visible = ((col < trunk_len) & (col < TRUNK)) | ((col >= TRUNK) & own)
    return (visible & (row_pos < row_len)).astype(f32)


def trunk_kernel(
    q_in, g_in, k_in, v_in, leaf_tree_in, leaf_len_in, trunk_len_in, w_key_ref, w_value_ref,
    dq_ref, dkv_ref, visible_ref, selector_ref, own_ref, give_ref,
    q_ref, g_ref, k_ref, v_ref, leaf_tree_ref, leaf_len_ref, trunk_len_ref,
    dq_buf, dkv_buf, visible_buf, selector_buf, give_buf, sems, out_sems, weight_sems,
):
    trunk = pl.ds(0, TRUNK)
    core = lax.axis_index("kvh") & 1
    chips, block = own_ref.shape[1:3]
    pairs = []
    for chip in range(chips):
        for ref, which in ((give_buf, 1 - core), (own_ref, core)):
            rows = pl.ds(pl.multiple_of((2 * chip + which) * block, block), block)
            pairs += [(w.at[rows, :], ref.at[part, chip]) for part, w in enumerate((w_key_ref, w_value_ref))]
    loads = copies(
        [
            (trunk_len_in, trunk_len_ref),
            (k_in.at[trunk, :], k_ref),
            (v_in.at[trunk, :], v_ref),
            (q_in.at[trunk, :], q_ref),
            (g_in.at[trunk, :], g_ref),
            (leaf_tree_in, leaf_tree_ref),
            (leaf_len_in, leaf_len_ref),
        ],
        sems,
    )
    weight_loads = copies(pairs, weight_sems)
    for load in loads:
        load.wait()
    seg = lax.axis_index("seg")
    trunk_len = trunk_len_ref[seg]
    keys = k_ref[...]
    values = v_ref[...]
    row = lax.broadcasted_iota(jnp.int32, (TRUNK, TRUNK), 0)
    col = lax.broadcasted_iota(jnp.int32, (TRUNK, TRUNK), 1)
    visible = (col <= row) & (row < trunk_len)
    for g in range(GROUP):
        head_q = q_ref[:, g * HEAD : (g + 1) * HEAD]
        head_g = g_ref[:, g * HEAD : (g + 1) * HEAD]
        scores = dot(head_q, keys, (1, 1)) * SCALE
        prob_grad = dot(head_g, values, (1, 1))
        probability, score_grad = softmax_grads(scores, prob_grad, visible)
        dq_buf[:, g * HEAD : (g + 1) * HEAD] = (dot(score_grad, keys, (1, 0)) * SCALE).astype(bf16)
        head_dk = dot(score_grad, head_q, (0, 0))
        head_dv = dot(probability, head_g, (0, 0))
        if g == 0:
            dkv_buf[:, 0:HEAD] = head_dk
            dkv_buf[:, HEAD:] = head_dv
        else:
            dkv_buf[:, 0:HEAD] += head_dk
            dkv_buf[:, HEAD:] += head_dv
    visible_buf[...] = leaf_visible(leaf_tree_ref, leaf_len_ref, trunk_len, seg)
    selector_buf[...] = leaf_selector(leaf_tree_ref, seg)
    for load in weight_loads:
        load.wait()
    stores = copies(
        [
            (dq_buf, dq_ref.at[trunk, :]),
            (dkv_buf, dkv_ref),
            (visible_buf, visible_ref),
            (selector_buf, selector_ref),
            (give_buf, give_ref),
        ],
        out_sems,
    )
    for store in stores:
        store.wait()


def leaf_kernel(
    in_ref, k_in, v_in, trunk_dkv_in, visible_in,
    out_ref, trunk_kv_ref, rows_ref, back_ref, dk_ref, dv_ref, out_buf, kv_buf,
    k_ref, v_ref, trunk_dkv_ref, visible_ref, sems, out_sems,
):
    trunk = pl.ds(0, TRUNK)
    loads = copies(
        [
            (k_in.at[trunk, :], k_ref),
            (v_in.at[trunk, :], v_ref),
            (visible_in, visible_ref),
            (trunk_dkv_in, trunk_dkv_ref),
        ],
        sems,
    )
    leaf_rows = visible_ref.shape[0]
    count = leaf_rows // LEAF
    rows_ref[...] = in_ref[...].astype(f32)

    def gather(tile):
        parts = [rows_ref[pl.ds(tile * LEAF + a, count, OUT_ROWS), :] for a in range(LEAF)]
        return jnp.concatenate(parts, axis=0).astype(bf16)

    for load in loads:
        load.wait()
    keys = jnp.concatenate([k_ref[...], gather(2 * GROUP)], axis=0)
    values = jnp.concatenate([v_ref[...], gather(2 * GROUP + 1)], axis=0)
    visible = visible_ref[...] > 0.5
    for g in range(GROUP):
        head_q = gather(g)
        head_g = gather(GROUP + g)
        scores = dot(head_q, keys, (1, 1)) * SCALE
        prob_grad = dot(head_g, values, (1, 1))
        probability, score_grad = softmax_grads(scores, prob_grad, visible)
        head_dq = dot(score_grad, keys, (1, 0)) * SCALE
        for a in range(LEAF):
            back_ref[pl.ds(g * LEAF + a, count, BACK_ROWS), :] = head_dq[a * count : (a + 1) * count, :]
        head_dk = dot(score_grad, head_q, (0, 0))
        head_dv = dot(probability, head_g, (0, 0))
        if g == 0:
            dk_ref[...] = head_dk
            dv_ref[...] = head_dv
        else:
            dk_ref[...] += head_dk
            dv_ref[...] += head_dv
    for a in range(LEAF):
        at = TRUNK + a * count
        back_ref[pl.ds(GROUP * LEAF + a, count, BACK_ROWS), :] = dk_ref[at : at + count, :] * SCALE
        back_ref[pl.ds((GROUP + 1) * LEAF + a, count, BACK_ROWS), :] = dv_ref[at : at + count, :]
    for spare in range(BACK_TILES * LEAF, BACK_ROWS):
        back_ref[pl.ds(spare, count, BACK_ROWS), :] = jnp.zeros((count, HEAD), f32)
    out_buf[...] = back_ref[...].astype(bf16)
    store = pltpu.make_async_copy(out_buf, out_ref, out_sems.at[0])
    store.start()
    kv_buf[:, 0:HEAD] = ((trunk_dkv_ref[:, 0:HEAD] + dk_ref[0:TRUNK, :]) * SCALE).astype(bf16)
    kv_buf[:, HEAD:] = (trunk_dkv_ref[:, HEAD:] + dv_ref[0:TRUNK, :]).astype(bf16)
    store_kv = pltpu.make_async_copy(kv_buf, trunk_kv_ref, out_sems.at[1])
    store_kv.start()
    store.wait()
    store_kv.wait()


def moved_tile(in_ref, rows_ref, selector, tile):
    count = in_ref.shape[0] // BACK_ROWS
    parts = [rows_ref[pl.ds(tile * LEAF + a, count, BACK_ROWS), :] for a in range(LEAF)]
    return dot(selector, jnp.concatenate(parts, axis=0).astype(bf16), (0, 0)).astype(bf16)


def leaf_kv_kernel(in_ref, selector_ref, after_ref, out_ref, rows_ref, selector_buf, kv_buf, sem, out_sem):
    load = pltpu.make_async_copy(selector_ref, selector_buf, sem)
    load.start()
    rows_ref[...] = in_ref[...].astype(f32)
    load.wait()
    for part in range(2):
        kv_buf[:, part * HEAD : (part + 1) * HEAD] = moved_tile(in_ref, rows_ref, selector_buf[...], GROUP + part)
    store = pltpu.make_async_copy(kv_buf, out_ref, out_sem)
    store.start()
    store.wait()


def leaf_query_kernel(in_ref, selector_ref, dq_in_ref, dq_ref, rows_ref, selector_buf, dq_buf, sem, out_sem):
    load = pltpu.make_async_copy(selector_ref, selector_buf, sem)
    load.start()
    rows_ref[...] = in_ref[...].astype(f32)
    load.wait()
    for tile in range(GROUP):
        dq_buf[:, tile * HEAD : (tile + 1) * HEAD] = moved_tile(in_ref, rows_ref, selector_buf[...], tile)
    store = pltpu.make_async_copy(dq_buf, dq_ref.at[pl.ds(TRUNK, dq_buf.shape[0]), :], out_sem)
    store.start()
    store.wait()


def chip_part(kv_ref, kv_other_ref, own_ref, other_ref, block):
    kv = jnp.concatenate([kv_ref[...], kv_other_ref[...]], axis=1)
    weight = jnp.concatenate([ref[part, block] for ref in (own_ref, other_ref) for part in range(2)], axis=1)
    return dot(weight, kv, (1, 1)).astype(bf16)


def send_parts(half, kv_ref, kv_other_ref, own_ref, other_ref, out_ref, buf, sems):
    stores = []
    for block in range(buf.shape[0]):
        buf[block] = chip_part(kv_ref, kv_other_ref, own_ref, other_ref, block)
        stores.append(pltpu.make_async_copy(buf.at[block], out_ref.at[block, half], sems.at[block]))
        stores[-1].start()
    for store in stores:
        store.wait()


def trunk_part_kernel(kv_ref, kv_other_ref, own_ref, other_ref, out_ref, token_ref, buf, sems):
    send_parts(0, kv_ref, kv_other_ref, own_ref, other_ref, out_ref, buf, sems)
    token_ref[...] = jnp.zeros(token_ref.shape, f32)


def leaf_part_kernel(kv_ref, kv_other_ref, own_ref, other_ref, parts_ref, out_ref, buf, sems):
    send_parts(1, kv_ref, kv_other_ref, own_ref, other_ref, out_ref, buf, sems)


def hidden_kernel(came_ref, out_ref):
    rows = came_ref.shape[3]
    for half in range(came_ref.shape[1]):
        total = came_ref[0, half].astype(f32)
        for chip in range(1, came_ref.shape[0]):
            total += came_ref[chip, half].astype(f32)
        out_ref[half * rows : (half + 1) * rows, :] = total.T.astype(bf16)


def call(kernel, outs, in_specs, out_specs, scratch=(), flops=0, moved=0, aliases={}, limit=24):
    return pl.pallas_call(
        kernel,
        out_shape=outs,
        in_specs=in_specs,
        out_specs=out_specs,
        scratch_shapes=list(scratch),
        input_output_aliases=aliases,
        compiler_params=pltpu.CompilerParams(vmem_limit_bytes=limit * 1024 * 1024),
        cost_estimate=pl.CostEstimate(flops=flops, bytes_accessed=moved, transcendentals=0),
    )


def shards(queries, key_rows, value_rows, grad_out, w_key, w_value, trunk_len, leaf_len, leaf_tree):
    count = lax.axis_size("seg")
    heads = lax.axis_size("kvh")
    chips = heads // 2
    leaf_rows = LEAF * count
    row_width = queries.shape[1]
    hidden = w_key.shape[0]
    columns = hidden // heads
    out = jax.ShapeDtypeStruct
    dma = pltpu.SemaphoreType.DMA

    vm = pltpu.VMEM

    send = call(
        send_kernel,
        out((count * OUT_ROWS, HEAD), bf16),
        [hbm] * 5,
        hbm,
        [
            vm((count, count), jnp.int32),
            vm((leaf_rows, row_width), bf16),
            vm((leaf_rows, row_width), bf16),
            vm((leaf_rows, HEAD), bf16),
            vm((leaf_rows, HEAD), bf16),
            vm((count * OUT_ROWS, HEAD), f32),
            vm((count * OUT_ROWS, HEAD), bf16),
            dma((5,)),
            dma,
        ],
        flops=10**8,
        moved=10**6,
        limit=60,
    )(queries, grad_out, key_rows, value_rows, leaf_tree)
    got = lax.all_to_all(
        send.reshape(count, OUT_ROWS, HEAD), "seg", split_axis=0, concat_axis=0, tiled=True
    ).reshape(count * OUT_ROWS, HEAD)

    keys_all = TRUNK + leaf_rows
    dq, trunk_dkv, visible, selector, own, give = call(
        trunk_kernel,
        [
            out(queries.shape, bf16),
            out((TRUNK, 2 * HEAD), f32),
            out((leaf_rows, keys_all), f32),
            out((leaf_rows, leaf_rows), bf16),
            out((2, chips, columns, HEAD), bf16),
            out((2, chips, columns, HEAD), bf16),
        ],
        [hbm] * 9,
        [hbm] * 4 + [vmem, hbm],
        [
            vm((TRUNK, row_width), bf16),
            vm((TRUNK, row_width), bf16),
            vm((TRUNK, HEAD), bf16),
            vm((TRUNK, HEAD), bf16),
            vm((count, count), jnp.int32),
            vm((count, count), jnp.int32),
            pltpu.SMEM((count,), jnp.int32),
            vm((TRUNK, row_width), bf16),
            vm((TRUNK, 2 * HEAD), f32),
            vm((leaf_rows, keys_all), f32),
            vm((leaf_rows, leaf_rows), bf16),
            vm((2, chips, columns, HEAD), bf16),
            dma((7,)),
            dma((5,)),
            dma((4 * chips,)),
        ],
        flops=4 * 10**10,
        moved=10**7,
        limit=60,
    )(queries, grad_out, key_rows, value_rows, leaf_tree, leaf_len, trunk_len, w_key, w_value)

    def swap(value):
        return lax.ppermute(value, "kvh", [(i, i ^ 1) for i in range(heads)])

    other = swap(give)

    back, trunk_kv = call(
        leaf_kernel,
        [out((count * BACK_ROWS, HEAD), bf16), out((TRUNK, 2 * HEAD), bf16)],
        [vmem] + [hbm] * 4,
        [hbm] * 2,
        [
            vm((count * OUT_ROWS, HEAD), f32),
            vm((count * BACK_ROWS, HEAD), f32),
            vm((keys_all, HEAD), f32),
            vm((keys_all, HEAD), f32),
            vm((count * BACK_ROWS, HEAD), bf16),
            vm((TRUNK, 2 * HEAD), bf16),
            vm((TRUNK, HEAD), bf16),
            vm((TRUNK, HEAD), bf16),
            vm((TRUNK, 2 * HEAD), f32),
            vm((leaf_rows, keys_all), f32),
            dma((4,)),
            dma((2,)),
        ],
        flops=4 * 10**10,
        moved=10**6,
    )(got, key_rows, value_rows, trunk_dkv, visible)

    part_flops = 2 * TRUNK * 4 * HEAD * chips * columns
    parts_shape = out((chips, 2, columns, TRUNK), bf16)
    parts_scratch = [vm((chips, columns, TRUNK), bf16), dma((chips,))]
    parts, token = call(
        trunk_part_kernel,
        [parts_shape, out((8, HEAD), f32)],
        [vmem] * 4,
        [hbm, vmem],
        parts_scratch,
        flops=part_flops,
        moved=4 * 10**6,
    )(trunk_kv, swap(trunk_kv), own, other)
    back = lax.all_to_all(
        back.reshape(count, BACK_ROWS, HEAD), "seg", split_axis=0, concat_axis=0, tiled=True
    ).reshape(count * BACK_ROWS, HEAD)
    leaf_kv = call(
        leaf_kv_kernel,
        out((leaf_rows, 2 * HEAD), bf16),
        [vmem, hbm, hbm],
        hbm,
        [
            vm((count * BACK_ROWS, HEAD), f32),
            vm((leaf_rows, leaf_rows), bf16),
            vm((leaf_rows, 2 * HEAD), bf16),
            dma,
            dma,
        ],
        flops=10**7,
        moved=10**6,
    )(back, selector, token)
    parts = call(
        leaf_part_kernel,
        parts_shape,
        [vmem] * 4 + [hbm],
        hbm,
        parts_scratch,
        flops=part_flops,
        moved=4 * 10**6,
        aliases={4: 0},
        limit=60,
    )(leaf_kv, swap(leaf_kv), own, other, parts)
    came = lax.all_to_all(
        parts,
        "kvh",
        split_axis=0,
        concat_axis=0,
        tiled=True,
        axis_index_groups=[[2 * x + c for x in range(chips)] for c in range(2)],
    )
    grad_query = call(
        leaf_query_kernel,
        out(queries.shape, bf16),
        [vmem, hbm, hbm],
        hbm,
        [
            vm((count * BACK_ROWS, HEAD), f32),
            vm((leaf_rows, leaf_rows), bf16),
            vm((leaf_rows, row_width), bf16),
            dma,
            dma,
        ],
        flops=10**8,
        moved=10**6,
        aliases={2: 0},
    )(back, selector, dq)
    grad_hidden = call(
        hidden_kernel,
        out((TRUNK + leaf_rows, columns), bf16),
        [vmem],
        vmem,
        flops=10**6,
        moved=10**6,
    )(came)
    return (grad_query, grad_hidden)


def solution(mesh):
    in_specs = (
        P("seg", "kvh"),
        P("seg", "kvh"),
        P("seg", "kvh"),
        P("seg", "kvh"),
        P(None, "kvh"),
        P(None, "kvh"),
        P(),
        P(),
        P(),
    )
    out_specs = (P("seg", "kvh"), P("seg", "kvh"))
    return jax.shard_map(shards, mesh=mesh, in_specs=in_specs, out_specs=out_specs, check_vma=False)
```

```python
import functools
import math

import jax
import jax.numpy as jnp
from jax import lax
from jax.experimental import pallas as pl
from jax.experimental.pallas import tpu as pltpu
from jax.sharding import PartitionSpec as P

GROUP = 5
TRUNK = 128
LEAF = 2
HEAD = 128
OUT_TILES = 2 * GROUP + 2
OUT_ROWS = OUT_TILES * LEAF
BACK_TILES = GROUP + 2
BACK_ROWS = 16
VERY_NEGATIVE = -1e30
SCALE = 1.0 / math.sqrt(HEAD)

f32 = jnp.float32
bf16 = jnp.bfloat16
vmem = pl.BlockSpec(memory_space=pltpu.VMEM)
smem = pl.BlockSpec(memory_space=pltpu.SMEM)
hbm = pl.BlockSpec(memory_space=pltpu.HBM)


def dot(a, b, contract):
    return lax.dot_general(a, b, ((contract[0:1], contract[1:2]), ((), ())), preferred_element_type=f32)


def leaf_selector(leaf_tree_ref, seg):
    count = leaf_tree_ref.shape[0]
    tree_row = leaf_tree_ref[pl.ds(seg, 1), :].astype(f32).astype(bf16)
    tree_rows = jnp.broadcast_to(tree_row, (16, count))
    leaf = lax.broadcasted_iota(jnp.int32, (count, LEAF * count), 0)
    col = lax.broadcasted_iota(jnp.int32, (count, LEAF * count), 1)
    repeat = (leaf == (col >> 1)).astype(f32).astype(bf16)
    tree_of_col = dot(tree_rows, repeat, (1, 0))[0:1, :].astype(jnp.int32)
    row = lax.broadcasted_iota(jnp.int32, (LEAF * count, LEAF * count), 0)
    col = lax.broadcasted_iota(jnp.int32, (LEAF * count, LEAF * count), 1)
    row_pos = (row >= count).astype(jnp.int32)
    hit = (tree_of_col == row - row_pos * count) & (row_pos == (col & 1))
    return hit.astype(f32).astype(bf16)


def copies(pairs, sems):
    started = [pltpu.make_async_copy(src, dst, sems.at[i]) for i, (src, dst) in enumerate(pairs)]
    for copy in started:
        copy.start()
    return started


def send_kernel(
    q_ref, g_ref, k_ref, v_ref, leaf_tree_ref,
    out_ref, tree_ref, q_buf, g_buf, k_buf, v_buf, rows_ref, out_buf, sems, out_sems,
):
    count = tree_ref.shape[0]
    leaves = pl.ds(TRUNK, LEAF * count)
    loads = [(leaf_tree_ref, tree_ref)]
    loads += [(src.at[leaves, :], dst) for src, dst in zip((q_ref, g_ref, k_ref, v_ref), (q_buf, g_buf, k_buf, v_buf))]
    loads = copies(loads, sems)
    seg = lax.axis_index("seg")
    loads[0].wait()
    selector = leaf_selector(tree_ref, seg)
    half = count // 2
    stores = []
    for part in range(2):
        at = part * half
        chosen = jnp.concatenate([selector[a * count + at : a * count + at + half, :] for a in range(LEAF)], axis=0)
        tile = 0
        for load, ref in zip(loads[1:], (q_buf, g_buf, k_buf, v_buf)):
            if part == 0:
                load.wait()
            moved = dot(chosen, ref[...], (1, 0))
            for column in range(0, ref.shape[1], HEAD):
                for a in range(LEAF):
                    rows_ref[pl.ds(at * OUT_ROWS + tile * LEAF + a, half, OUT_ROWS), :] = moved[
                        a * half : (a + 1) * half, column : column + HEAD
                    ]
                tile += 1
        rows = pl.ds(at * OUT_ROWS, half * OUT_ROWS)
        out_buf[rows, :] = rows_ref[rows, :].astype(bf16)
        stores.append(pltpu.make_async_copy(out_buf.at[rows, :], out_ref.at[rows, :], out_sems.at[part]))
        stores[-1].start()
    for store in stores:
        store.wait()


def softmax_grads(scores, prob_grad, visible):
    masked = jnp.where(visible, scores, VERY_NEGATIVE)
    row_max = jnp.max(masked, axis=-1, keepdims=True)
    weights = jnp.where(visible, jnp.exp(masked - row_max), 0.0)
    row_total = jnp.maximum(jnp.sum(weights, axis=-1, keepdims=True), 1.0)
    probability = weights * (1.0 / row_total)
    row_delta = jnp.sum(probability * prob_grad, axis=-1, keepdims=True)
    score_grad = (probability * (prob_grad - row_delta)).astype(bf16)
    return probability.astype(bf16), score_grad


def leaf_visible(leaf_tree_ref, leaf_len_ref, trunk_len, seg):
    count = leaf_tree_ref.shape[0]
    in_len = jnp.sum(jnp.where(leaf_tree_ref[...] == seg, leaf_len_ref[...], 0), axis=1, keepdims=True)
    row_len = jnp.concatenate([in_len] * LEAF, axis=0)
    leaf_rows = LEAF * count
    shape = (leaf_rows, TRUNK + leaf_rows)
    row = lax.broadcasted_iota(jnp.int32, shape, 0)
    col = lax.broadcasted_iota(jnp.int32, shape, 1)
    row_pos = (row >= count).astype(jnp.int32)
    leaf_col = col - TRUNK
    col_pos = (leaf_col >= count).astype(jnp.int32)
    own = (row - row_pos * count == leaf_col - col_pos * count) & (col_pos <= row_pos)
    visible = ((col < trunk_len) & (col < TRUNK)) | ((col >= TRUNK) & own)
    return visible & (row_pos < row_len)


def trunk_kernel(
    q_in, g_in, k_in, v_in, trunk_len_in, w_key_ref, w_value_ref,
    dq_ref, dkv_ref, own_ref, give_ref,
    q_ref, g_ref, k_ref, v_ref, trunk_len_ref, dq_buf, dkv_buf, give_buf, sems, out_sems, weight_sems,
):
    trunk = pl.ds(0, TRUNK)
    core = lax.axis_index("kvh") & 1
    chips, block = own_ref.shape[1:3]
    pairs = []
    for chip in range(chips):
        for ref, which in ((give_buf, 1 - core), (own_ref, core)):
            rows = pl.ds(pl.multiple_of((2 * chip + which) * block, block), block)
            pairs += [(w.at[rows, :], ref.at[part, chip]) for part, w in enumerate((w_key_ref, w_value_ref))]
    loads = copies(
        [
            (trunk_len_in, trunk_len_ref),
            (k_in.at[trunk, :], k_ref),
            (v_in.at[trunk, :], v_ref),
            (q_in.at[trunk, :], q_ref),
            (g_in.at[trunk, :], g_ref),
        ],
        sems,
    )
    weight_loads = copies(pairs, weight_sems)
    for load in loads:
        load.wait()
    seg = lax.axis_index("seg")
    trunk_len = trunk_len_ref[seg]
    keys = k_ref[...]
    values = v_ref[...]
    row = lax.broadcasted_iota(jnp.int32, (TRUNK, TRUNK), 0)
    col = lax.broadcasted_iota(jnp.int32, (TRUNK, TRUNK), 1)
    visible = (col <= row) & (row < trunk_len)
    for g in range(GROUP):
        head_q = q_ref[:, g * HEAD : (g + 1) * HEAD]
        head_g = g_ref[:, g * HEAD : (g + 1) * HEAD]
        scores = dot(head_q, keys, (1, 1)) * SCALE
        prob_grad = dot(head_g, values, (1, 1))
        probability, score_grad = softmax_grads(scores, prob_grad, visible)
        dq_buf[:, g * HEAD : (g + 1) * HEAD] = (dot(score_grad, keys, (1, 0)) * SCALE).astype(bf16)
        head_dk = dot(score_grad, head_q, (0, 0))
        head_dv = dot(probability, head_g, (0, 0))
        if g == 0:
            dkv_buf[:, 0:HEAD] = head_dk
            dkv_buf[:, HEAD:] = head_dv
        else:
            dkv_buf[:, 0:HEAD] += head_dk
            dkv_buf[:, HEAD:] += head_dv
    dkv_buf[:, 0:HEAD] *= SCALE
    for load in weight_loads:
        load.wait()
    stores = copies(
        [
            (dq_buf, dq_ref.at[trunk, :]),
            (dkv_buf, dkv_ref),
            (give_buf, give_ref),
        ],
        out_sems,
    )
    for store in stores:
        store.wait()


def leaf_kernel(
    in_ref, k_ref, v_ref, leaf_tree_ref, leaf_len_ref, trunk_len_in,
    out_ref, dkv_ref, rows_ref, back_ref, q_buf, g_buf, ds_buf, p_buf, out_buf, trunk_len_ref, sem, out_sem,
):
    load = pltpu.make_async_copy(trunk_len_in, trunk_len_ref, sem)
    load.start()
    count = leaf_tree_ref.shape[0]
    leaf_rows = LEAF * count
    rows_ref[...] = in_ref[...].astype(f32)

    def gather(tile):
        parts = [rows_ref[pl.ds(tile * LEAF + a, count, OUT_ROWS), :] for a in range(LEAF)]
        return jnp.concatenate(parts, axis=0).astype(bf16)

    keys = jnp.concatenate([k_ref[0:TRUNK, :], gather(2 * GROUP)], axis=0)
    values = jnp.concatenate([v_ref[0:TRUNK, :], gather(2 * GROUP + 1)], axis=0)
    seg = lax.axis_index("seg")
    load.wait()
    visible = leaf_visible(leaf_tree_ref, leaf_len_ref, trunk_len_ref[seg], seg)
    for g in range(GROUP):
        rows = slice(g * leaf_rows, (g + 1) * leaf_rows)
        head_q = gather(g)
        head_g = gather(GROUP + g)
        q_buf[rows, :] = head_q
        g_buf[rows, :] = head_g
        scores = dot(head_q, keys, (1, 1)) * SCALE
        prob_grad = dot(head_g, values, (1, 1))
        p_buf[rows, :], ds_buf[rows, :] = softmax_grads(scores, prob_grad, visible)
    query_grad = dot(ds_buf[...], keys, (1, 0)) * SCALE
    for g in range(GROUP):
        for a in range(LEAF):
            at = g * leaf_rows + a * count
            back_ref[pl.ds(g * LEAF + a, count, BACK_ROWS), :] = query_grad[at : at + count, :]
    key_grad = dot(ds_buf[...], q_buf[...], (0, 0)) * SCALE
    value_grad = dot(p_buf[...], g_buf[...], (0, 0))
    for a in range(LEAF):
        at = TRUNK + a * count
        back_ref[pl.ds(GROUP * LEAF + a, count, BACK_ROWS), :] = key_grad[at : at + count, :]
        back_ref[pl.ds((GROUP + 1) * LEAF + a, count, BACK_ROWS), :] = value_grad[at : at + count, :]
    leaf = lax.broadcasted_iota(jnp.int32, (count, count), 1)
    number = jnp.sum(jnp.where(leaf_tree_ref[...] == seg, leaf, 0), axis=1, keepdims=True).astype(f32)
    for spare in range(BACK_TILES * LEAF, BACK_ROWS):
        back_ref[pl.ds(spare, count, BACK_ROWS), :] = jnp.broadcast_to(number, (count, HEAD))
    out_buf[...] = back_ref[...].astype(bf16)
    store = pltpu.make_async_copy(out_buf, out_ref, out_sem)
    store.start()
    dkv_ref[:, 0:HEAD] = key_grad[0:TRUNK, :]
    dkv_ref[:, HEAD:] = value_grad[0:TRUNK, :]
    store.wait()


def back_selector(rows_ref):
    count = rows_ref.shape[0] // BACK_ROWS
    number = rows_ref[pl.ds(BACK_TILES * LEAF, count, BACK_ROWS), :].astype(jnp.int32)
    col = lax.broadcasted_iota(jnp.int32, number.shape, 1)
    hits = [((number == (col >> 1)) & ((col & 1) == a)).astype(f32) for a in range(LEAF)]
    return jnp.concatenate(hits, axis=0)[:, 0 : LEAF * count].astype(bf16)


def moved_tile(rows_ref, selector, tile):
    count = rows_ref.shape[0] // BACK_ROWS
    parts = [rows_ref[pl.ds(tile * LEAF + a, count, BACK_ROWS), :] for a in range(LEAF)]
    return dot(selector, jnp.concatenate(parts, axis=0).astype(bf16), (0, 0)).astype(bf16)


def leaf_kv_kernel(in_ref, after_ref, out_ref, rows_ref):
    rows_ref[...] = in_ref[...].astype(f32)
    selector = back_selector(rows_ref)
    for part in range(2):
        out_ref[:, part * HEAD : (part + 1) * HEAD] = moved_tile(rows_ref, selector, GROUP + part)


def leaf_query_kernel(in_ref, dq_in_ref, dq_ref, token_ref, rows_ref, dq_buf, sem):
    rows_ref[...] = in_ref[...].astype(f32)
    selector = back_selector(rows_ref)
    for tile in range(GROUP):
        dq_buf[:, tile * HEAD : (tile + 1) * HEAD] = moved_tile(rows_ref, selector, tile)
    store = pltpu.make_async_copy(dq_buf, dq_ref.at[pl.ds(TRUNK, dq_buf.shape[0]), :], sem)
    store.start()
    token_ref[...] = jnp.zeros(token_ref.shape, f32)
    store.wait()


def chip_part(kv_ref, kv_other_ref, own_ref, other_ref, block):
    kv = jnp.concatenate([kv_ref[...], kv_other_ref[...]], axis=1)
    weight = jnp.concatenate([ref[part, block] for ref in (own_ref, other_ref) for part in range(2)], axis=1)
    return dot(weight, kv, (1, 1)).astype(bf16)


def trunk_part_kernel(kv_ref, kv_other_ref, own_ref, other_ref, *refs):
    chips = own_ref.shape[1]
    outs, token_ref, buf, sems = refs[:chips], refs[chips], refs[-2], refs[-1]
    chip = lax.axis_index("kvh") >> 1
    stores = []
    for step in reversed(range(chips)):
        buf[step] = chip_part(kv_ref, kv_other_ref, own_ref, other_ref, lax.rem(chip + step, chips))
        stores.append(pltpu.make_async_copy(buf.at[step], outs[step], sems.at[step]))
        stores[-1].start()
    token_ref[...] = jnp.zeros(token_ref.shape, f32)
    for store in stores:
        store.wait()


def leaf_part_kernel(kv_ref, kv_other_ref, own_ref, other_ref, after_ref, *refs):
    out_ref = refs[-1]
    for block in range(out_ref.shape[0]):
        out_ref[block] = chip_part(kv_ref, kv_other_ref, own_ref, other_ref, block)


def hidden_kernel(leaf_ref, *refs):
    trunk_refs, (out_ref, buf, sems) = refs[:-3], refs[-3:]
    stores = []
    for i, parts in enumerate(([ref[...] for ref in trunk_refs], [leaf_ref[chip] for chip in range(leaf_ref.shape[0])])):
        total = parts[0].astype(f32)
        for part in parts[1:]:
            total += part.astype(f32)
        rows = pl.ds(i * TRUNK, TRUNK)
        buf[rows, :] = total.T.astype(bf16)
        stores.append(pltpu.make_async_copy(buf.at[rows, :], out_ref.at[rows, :], sems.at[i]))
        stores[-1].start()
    for store in stores:
        store.wait()


def call(kernel, outs, in_specs, out_specs, scratch=(), flops=0, moved=0, aliases={}, limit=24):
    return pl.pallas_call(
        kernel,
        out_shape=outs,
        in_specs=in_specs,
        out_specs=out_specs,
        scratch_shapes=list(scratch),
        input_output_aliases=aliases,
        compiler_params=pltpu.CompilerParams(vmem_limit_bytes=limit * 1024 * 1024),
        cost_estimate=pl.CostEstimate(flops=flops, bytes_accessed=moved, transcendentals=0),
    )


def shards(queries, key_rows, value_rows, grad_out, w_key, w_value, trunk_len, leaf_len, leaf_tree):
    count = lax.axis_size("seg")
    heads = lax.axis_size("kvh")
    chips = heads // 2
    leaf_rows = LEAF * count
    row_width = queries.shape[1]
    hidden = w_key.shape[0]
    columns = hidden // heads
    out = jax.ShapeDtypeStruct
    dma = pltpu.SemaphoreType.DMA

    vm = pltpu.VMEM

    send = call(
        send_kernel,
        out((count * OUT_ROWS, HEAD), bf16),
        [hbm] * 5,
        hbm,
        [
            vm((count, count), jnp.int32),
            vm((leaf_rows, row_width), bf16),
            vm((leaf_rows, row_width), bf16),
            vm((leaf_rows, HEAD), bf16),
            vm((leaf_rows, HEAD), bf16),
            vm((count * OUT_ROWS, HEAD), f32),
            vm((count * OUT_ROWS, HEAD), bf16),
            dma((5,)),
            dma((2,)),
        ],
        flops=10**8,
        moved=10**6,
        limit=60,
    )(queries, grad_out, key_rows, value_rows, leaf_tree)
    got = lax.all_to_all(
        send.reshape(count, OUT_ROWS, HEAD), "seg", split_axis=0, concat_axis=0, tiled=True
    ).reshape(count * OUT_ROWS, HEAD)

    keys_all = TRUNK + leaf_rows
    dq, trunk_dkv, own, give = call(
        trunk_kernel,
        [
            out(queries.shape, bf16),
            out((TRUNK, 2 * HEAD), f32),
            out((2, chips, columns, HEAD), bf16),
            out((2, chips, columns, HEAD), bf16),
        ],
        [hbm] * 7,
        [hbm] * 2 + [vmem, hbm],
        [
            vm((TRUNK, row_width), bf16),
            vm((TRUNK, row_width), bf16),
            vm((TRUNK, HEAD), bf16),
            vm((TRUNK, HEAD), bf16),
            pltpu.SMEM((count,), jnp.int32),
            vm((TRUNK, row_width), bf16),
            vm((TRUNK, 2 * HEAD), f32),
            vm((2, chips, columns, HEAD), bf16),
            dma((5,)),
            dma((3,)),
            dma((4 * chips,)),
        ],
        flops=4 * 10**10,
        moved=10**7,
        limit=60,
    )(queries, grad_out, key_rows, value_rows, trunk_len, w_key, w_value)

    def swap(value):
        return lax.ppermute(value, "kvh", [(i, i ^ 1) for i in range(heads)])

    other = swap(give)

    back, leaf_dkv = call(
        leaf_kernel,
        [out((count * BACK_ROWS, HEAD), bf16), out((TRUNK, 2 * HEAD), f32)],
        [vmem] * 5 + [hbm],
        [hbm, vmem],
        [
            vm((count * OUT_ROWS, HEAD), f32),
            vm((count * BACK_ROWS, HEAD), f32),
            vm((GROUP * leaf_rows, HEAD), bf16),
            vm((GROUP * leaf_rows, HEAD), bf16),
            vm((GROUP * leaf_rows, keys_all), bf16),
            vm((GROUP * leaf_rows, keys_all), bf16),
            vm((count * BACK_ROWS, HEAD), bf16),
            pltpu.SMEM((count,), jnp.int32),
            dma,
            dma,
        ],
        flops=4 * 10**10,
        moved=10**6,
    )(got, key_rows, value_rows, leaf_tree, leaf_len, trunk_len)
    trunk_kv = (trunk_dkv + leaf_dkv).astype(bf16)

    part_flops = 2 * TRUNK * 4 * HEAD * chips * columns
    part_shape = (columns, TRUNK)
    *trunk_parts, token = call(
        trunk_part_kernel,
        [out(part_shape, bf16)] * chips + [out((8, HEAD), f32)],
        [vmem] * 4,
        [hbm] * chips + [vmem],
        [vm((chips,) + part_shape, bf16), dma((chips,))],
        flops=part_flops,
        moved=4 * 10**6,
    )(trunk_kv, swap(trunk_kv), own, other)
    trunk_came = [trunk_parts[0]]
    for step in (2, 1, 3):
        route = [(2 * x + c, 2 * ((x + step) % chips) + c) for x in range(chips) for c in range(2)]
        trunk_came.append(lax.ppermute(trunk_parts[step], "kvh", route))
    back = lax.all_to_all(
        back.reshape(count, BACK_ROWS, HEAD), "seg", split_axis=0, concat_axis=0, tiled=True
    ).reshape(count * BACK_ROWS, HEAD)
    leaf_kv = call(
        leaf_kv_kernel,
        out((leaf_rows, 2 * HEAD), bf16),
        [vmem] * 2,
        vmem,
        [vm((count * BACK_ROWS, HEAD), f32)],
        flops=4 * 10**10,
        moved=10**6,
    )(back, token)
    grad_query, token = call(
        leaf_query_kernel,
        [out(queries.shape, bf16), out((8, HEAD), f32)],
        [vmem, hbm],
        [hbm, vmem],
        [vm((count * BACK_ROWS, HEAD), f32), vm((leaf_rows, row_width), bf16), dma],
        flops=10**8,
        moved=10**6,
        aliases={1: 0},
    )(back, dq)
    parts = call(
        leaf_part_kernel,
        out((chips, columns, leaf_rows), bf16),
        [vmem] * 5 + [hbm] * (chips - 1),
        vmem,
        flops=4 * 10**10,
        moved=4 * 10**6,
    )(leaf_kv, swap(leaf_kv), own, other, token, *trunk_came[1:])
    came = lax.all_to_all(
        parts,
        "kvh",
        split_axis=0,
        concat_axis=0,
        tiled=True,
        axis_index_groups=[[2 * x + c for x in range(chips)] for c in range(2)],
    )
    grad_hidden = call(
        hidden_kernel,
        out((TRUNK + leaf_rows, columns), bf16),
        [vmem] * (1 + chips),
        hbm,
        [vm((TRUNK + leaf_rows, columns), bf16), dma((2,))],
        flops=10**6,
        moved=10**6,
    )(came, *trunk_came)
    return (grad_query, grad_hidden)


def solution(mesh):
    in_specs = (
        P("seg", "kvh"),
        P("seg", "kvh"),
        P("seg", "kvh"),
        P("seg", "kvh"),
        P(None, "kvh"),
        P(None, "kvh"),
        P(),
        P(),
        P(),
    )
    out_specs = (P("seg", "kvh"), P("seg", "kvh"))
    return jax.shard_map(shards, mesh=mesh, in_specs=in_specs, out_specs=out_specs, check_vma=False)
```

```python
import functools
import math

import jax
import jax.numpy as jnp
from jax import lax
from jax.experimental import pallas as pl
from jax.experimental.pallas import tpu as pltpu
from jax.sharding import PartitionSpec as P

GROUP = 5
TRUNK = 128
LEAF = 2
HEAD = 128
OUT_TILES = 2 * GROUP + 2
OUT_ROWS = OUT_TILES * LEAF
BACK_TILES = GROUP + 2
BACK_ROWS = 16
VERY_NEGATIVE = -1e30
SCALE = 1.0 / math.sqrt(HEAD)

f32 = jnp.float32
bf16 = jnp.bfloat16
vmem = pl.BlockSpec(memory_space=pltpu.VMEM)
smem = pl.BlockSpec(memory_space=pltpu.SMEM)
hbm = pl.BlockSpec(memory_space=pltpu.HBM)


def dot(a, b, contract):
    return lax.dot_general(a, b, ((contract[0:1], contract[1:2]), ((), ())), preferred_element_type=f32)


def leaf_selector(leaf_tree_ref, seg):
    count = leaf_tree_ref.shape[0]
    tree_row = leaf_tree_ref[pl.ds(seg, 1), :].astype(f32).astype(bf16)
    tree_rows = jnp.broadcast_to(tree_row, (16, count))
    leaf = lax.broadcasted_iota(jnp.int32, (count, LEAF * count), 0)
    col = lax.broadcasted_iota(jnp.int32, (count, LEAF * count), 1)
    repeat = (leaf == (col >> 1)).astype(f32).astype(bf16)
    tree_of_col = dot(tree_rows, repeat, (1, 0))[0:1, :].astype(jnp.int32)
    row = lax.broadcasted_iota(jnp.int32, (LEAF * count, LEAF * count), 0)
    col = lax.broadcasted_iota(jnp.int32, (LEAF * count, LEAF * count), 1)
    row_pos = (row >= count).astype(jnp.int32)
    hit = (tree_of_col == row - row_pos * count) & (row_pos == (col & 1))
    return hit.astype(f32).astype(bf16)


def copies(pairs, sems):
    started = [pltpu.make_async_copy(src, dst, sems.at[i]) for i, (src, dst) in enumerate(pairs)]
    for copy in started:
        copy.start()
    return started


def send_kernel(
    q_ref, g_ref, k_ref, v_ref, leaf_tree_ref,
    out_ref, tree_ref, q_buf, g_buf, k_buf, v_buf, rows_ref, out_buf, sems, out_sems,
):
    count = tree_ref.shape[0]
    leaves = pl.ds(TRUNK, LEAF * count)
    loads = [(leaf_tree_ref, tree_ref)]
    loads += [(src.at[leaves, :], dst) for src, dst in zip((q_ref, g_ref, k_ref, v_ref), (q_buf, g_buf, k_buf, v_buf))]
    loads = copies(loads, sems)
    seg = lax.axis_index("seg")
    loads[0].wait()
    selector = leaf_selector(tree_ref, seg)
    half = count // 2
    stores = []
    for part in range(2):
        at = part * half
        chosen = jnp.concatenate([selector[a * count + at : a * count + at + half, :] for a in range(LEAF)], axis=0)
        tile = 0
        for load, ref in zip(loads[1:], (q_buf, g_buf, k_buf, v_buf)):
            if part == 0:
                load.wait()
            moved = dot(chosen, ref[...], (1, 0))
            for column in range(0, ref.shape[1], HEAD):
                for a in range(LEAF):
                    rows_ref[pl.ds(at * OUT_ROWS + tile * LEAF + a, half, OUT_ROWS), :] = moved[
                        a * half : (a + 1) * half, column : column + HEAD
                    ]
                tile += 1
        rows = pl.ds(at * OUT_ROWS, half * OUT_ROWS)
        out_buf[rows, :] = rows_ref[rows, :].astype(bf16)
        stores.append(pltpu.make_async_copy(out_buf.at[rows, :], out_ref.at[rows, :], out_sems.at[part]))
        stores[-1].start()
    for store in stores:
        store.wait()


def softmax_grads(scores, prob_grad, visible):
    masked = jnp.where(visible, scores, VERY_NEGATIVE)
    row_max = jnp.max(masked, axis=-1, keepdims=True)
    weights = jnp.where(visible, jnp.exp(masked - row_max), 0.0)
    row_total = jnp.maximum(jnp.sum(weights, axis=-1, keepdims=True), 1.0)
    probability = weights * (1.0 / row_total)
    row_delta = jnp.sum(probability * prob_grad, axis=-1, keepdims=True)
    score_grad = (probability * (prob_grad - row_delta)).astype(bf16)
    return probability.astype(bf16), score_grad


def leaf_visible(leaf_tree_ref, leaf_len_ref, trunk_len, seg):
    count = leaf_tree_ref.shape[0]
    in_len = jnp.sum(jnp.where(leaf_tree_ref[...] == seg, leaf_len_ref[...], 0), axis=1, keepdims=True)
    row_len = jnp.concatenate([in_len] * LEAF, axis=0)
    leaf_rows = LEAF * count
    shape = (leaf_rows, TRUNK + leaf_rows)
    row = lax.broadcasted_iota(jnp.int32, shape, 0)
    col = lax.broadcasted_iota(jnp.int32, shape, 1)
    row_pos = (row >= count).astype(jnp.int32)
    leaf_col = col - TRUNK
    col_pos = (leaf_col >= count).astype(jnp.int32)
    own = (row - row_pos * count == leaf_col - col_pos * count) & (col_pos <= row_pos)
    visible = ((col < trunk_len) & (col < TRUNK)) | ((col >= TRUNK) & own)
    return visible & (row_pos < row_len)


def weight_pairs(w_key_ref, w_value_ref, to_ref, core):
    chips, block = to_ref.shape[1:3]
    pairs = []
    for chip in range(chips):
        rows = pl.ds(pl.multiple_of((2 * chip + core) * block, block), block)
        pairs += [(w.at[rows, :], to_ref.at[part, chip]) for part, w in enumerate((w_key_ref, w_value_ref))]
    return pairs


def trunk_kernel(
    q_in, g_in, k_in, v_in, trunk_len_in, w_key_ref, w_value_ref,
    dq_ref, dkv_ref, own_ref, give_ref,
    q_ref, g_ref, k_ref, v_ref, trunk_len_ref, ds_buf, p_buf, dq_buf, dkv_buf, give_buf,
    sems, out_sems, own_sems, give_sems, gave_sems,
):
    trunk = pl.ds(0, TRUNK)
    core = lax.axis_index("kvh") & 1
    chips = own_ref.shape[1]
    loads = copies(
        [
            (trunk_len_in, trunk_len_ref),
            (k_in.at[trunk, :], k_ref),
            (v_in.at[trunk, :], v_ref),
            (q_in.at[trunk, :], q_ref),
            (g_in.at[trunk, :], g_ref),
        ],
        sems,
    )
    give_loads = copies(weight_pairs(w_key_ref, w_value_ref, give_buf, 1 - core), give_sems)
    own_loads = copies(weight_pairs(w_key_ref, w_value_ref, own_ref, core), own_sems)
    for load in loads:
        load.wait()
    trunk_len = trunk_len_ref[lax.axis_index("seg")]
    keys = k_ref[...]
    values = v_ref[...]
    row = lax.broadcasted_iota(jnp.int32, (TRUNK, TRUNK), 0)
    col = lax.broadcasted_iota(jnp.int32, (TRUNK, TRUNK), 1)
    visible = (col <= row) & (row < trunk_len)
    stores = []
    for g in range(GROUP):
        columns = slice(g * HEAD, (g + 1) * HEAD)
        rows = slice(g * TRUNK, (g + 1) * TRUNK)
        scores = dot(q_ref[:, columns], keys, (1, 1)) * SCALE
        prob_grad = dot(g_ref[:, columns], values, (1, 1))
        p_buf[rows, :], ds_buf[rows, :] = softmax_grads(scores, prob_grad, visible)
        if g == 1:
            for i, load in enumerate(give_loads):
                load.wait()
                part, chip = i % 2, i // 2
                stores += copies([(give_buf.at[part, chip], give_ref.at[part, chip])], gave_sems.at[pl.ds(i, 1)])
    query_grad = dot(ds_buf[...], keys, (1, 0)) * SCALE
    for g in range(GROUP):
        dq_buf[:, g * HEAD : (g + 1) * HEAD] = query_grad[g * TRUNK : (g + 1) * TRUNK, :].astype(bf16)
    head_q = jnp.concatenate([q_ref[:, g * HEAD : (g + 1) * HEAD] for g in range(GROUP)], axis=0)
    head_g = jnp.concatenate([g_ref[:, g * HEAD : (g + 1) * HEAD] for g in range(GROUP)], axis=0)
    dkv_buf[:, 0:HEAD] = dot(ds_buf[...], head_q, (0, 0)) * SCALE
    dkv_buf[:, HEAD:] = dot(p_buf[...], head_g, (0, 0))
    stores += copies([(dq_buf, dq_ref.at[trunk, :]), (dkv_buf, dkv_ref)], out_sems)
    for copy in stores + own_loads:
        copy.wait()


def leaf_kernel(
    in_ref, k_ref, v_ref, leaf_tree_ref, leaf_len_ref, trunk_len_in,
    out_ref, dkv_ref, rows_ref, back_ref, q_buf, g_buf, ds_buf, p_buf, out_buf, trunk_len_ref, sem, out_sem,
):
    load = pltpu.make_async_copy(trunk_len_in, trunk_len_ref, sem)
    load.start()
    count = leaf_tree_ref.shape[0]
    leaf_rows = LEAF * count
    rows_ref[...] = in_ref[...].astype(f32)

    def gather(tile):
        parts = [rows_ref[pl.ds(tile * LEAF + a, count, OUT_ROWS), :] for a in range(LEAF)]
        return jnp.concatenate(parts, axis=0).astype(bf16)

    keys = jnp.concatenate([k_ref[0:TRUNK, :], gather(2 * GROUP)], axis=0)
    values = jnp.concatenate([v_ref[0:TRUNK, :], gather(2 * GROUP + 1)], axis=0)
    seg = lax.axis_index("seg")
    load.wait()
    visible = leaf_visible(leaf_tree_ref, leaf_len_ref, trunk_len_ref[seg], seg)
    for g in range(GROUP):
        rows = slice(g * leaf_rows, (g + 1) * leaf_rows)
        head_q = gather(g)
        head_g = gather(GROUP + g)
        q_buf[rows, :] = head_q
        g_buf[rows, :] = head_g
        scores = dot(head_q, keys, (1, 1)) * SCALE
        prob_grad = dot(head_g, values, (1, 1))
        p_buf[rows, :], ds_buf[rows, :] = softmax_grads(scores, prob_grad, visible)
    query_grad = dot(ds_buf[...], keys, (1, 0)) * SCALE
    for g in range(GROUP):
        for a in range(LEAF):
            at = g * leaf_rows + a * count
            back_ref[pl.ds(g * LEAF + a, count, BACK_ROWS), :] = query_grad[at : at + count, :]
    key_grad = dot(ds_buf[...], q_buf[...], (0, 0)) * SCALE
    value_grad = dot(p_buf[...], g_buf[...], (0, 0))
    for a in range(LEAF):
        at = TRUNK + a * count
        back_ref[pl.ds(GROUP * LEAF + a, count, BACK_ROWS), :] = key_grad[at : at + count, :]
        back_ref[pl.ds((GROUP + 1) * LEAF + a, count, BACK_ROWS), :] = value_grad[at : at + count, :]
    leaf = lax.broadcasted_iota(jnp.int32, (count, count), 1)
    number = jnp.sum(jnp.where(leaf_tree_ref[...] == seg, leaf, 0), axis=1, keepdims=True).astype(f32)
    for spare in range(BACK_TILES * LEAF, BACK_ROWS):
        back_ref[pl.ds(spare, count, BACK_ROWS), :] = jnp.broadcast_to(number, (count, HEAD))
    out_buf[...] = back_ref[...].astype(bf16)
    store = pltpu.make_async_copy(out_buf, out_ref, out_sem)
    store.start()
    dkv_ref[:, 0:HEAD] = key_grad[0:TRUNK, :]
    dkv_ref[:, HEAD:] = value_grad[0:TRUNK, :]
    store.wait()


def back_selector(rows_ref):
    count = rows_ref.shape[0] // BACK_ROWS
    number = rows_ref[pl.ds(BACK_TILES * LEAF, count, BACK_ROWS), :].astype(jnp.int32)
    col = lax.broadcasted_iota(jnp.int32, number.shape, 1)
    hits = [((number == (col >> 1)) & ((col & 1) == a)).astype(f32) for a in range(LEAF)]
    return jnp.concatenate(hits, axis=0)[:, 0 : LEAF * count].astype(bf16)


def moved_tile(rows_ref, selector, tile):
    count = rows_ref.shape[0] // BACK_ROWS
    parts = [rows_ref[pl.ds(tile * LEAF + a, count, BACK_ROWS), :] for a in range(LEAF)]
    return dot(selector, jnp.concatenate(parts, axis=0).astype(bf16), (0, 0)).astype(bf16)


def leaf_kv_kernel(in_ref, after_ref, out_ref, rows_ref):
    rows_ref[...] = in_ref[...].astype(f32)
    selector = back_selector(rows_ref)
    for part in range(2):
        out_ref[:, part * HEAD : (part + 1) * HEAD] = moved_tile(rows_ref, selector, GROUP + part)


def leaf_query_kernel(in_ref, dq_in_ref, dq_ref, token_ref, rows_ref, dq_buf, sem):
    rows_ref[...] = in_ref[...].astype(f32)
    selector = back_selector(rows_ref)
    for tile in range(GROUP):
        dq_buf[:, tile * HEAD : (tile + 1) * HEAD] = moved_tile(rows_ref, selector, tile)
    store = pltpu.make_async_copy(dq_buf, dq_ref.at[pl.ds(TRUNK, dq_buf.shape[0]), :], sem)
    store.start()
    token_ref[...] = jnp.zeros(token_ref.shape, f32)
    store.wait()


def chip_part(kv_ref, kv_other_ref, own_ref, other_ref, block):
    kv = jnp.concatenate([kv_ref[...], kv_other_ref[...]], axis=1)
    weight = jnp.concatenate([ref[part, block] for ref in (own_ref, other_ref) for part in range(2)], axis=1)
    return dot(weight, kv, (1, 1)).astype(bf16)


def trunk_part_kernel(steps, kv_ref, kv_other_ref, own_ref, other_ref, *refs):
    count = len(steps[0]) + 1
    chips = own_ref.shape[1]
    outs, token_ref, buf, sems = refs[:count], refs[count], refs[-2], refs[-1]
    kvh = lax.axis_index("kvh")
    chip, core = kvh >> 1, kvh & 1
    stores = []
    for i, (even, odd) in enumerate(zip(steps[0] + (0,), steps[1] + (0,))):
        block = lax.rem(chip + even + core * (odd - even), chips)
        buf[i] = chip_part(kv_ref, kv_other_ref, own_ref, other_ref, block)
        stores.append(pltpu.make_async_copy(buf.at[i], outs[i], sems.at[i]))
        stores[-1].start()
    token_ref[...] = jnp.zeros(token_ref.shape, f32)
    for store in stores:
        store.wait()


def leaf_part_kernel(kv_ref, kv_other_ref, own_ref, other_ref, after_ref, out_ref):
    for block in range(out_ref.shape[0]):
        out_ref[block] = chip_part(kv_ref, kv_other_ref, own_ref, other_ref, block)


def hidden_kernel(leaf_ref, *refs):
    trunk_refs, (out_ref, buf, sems) = refs[:-3], refs[-3:]
    stores = []
    for i, parts in enumerate(([ref[...] for ref in trunk_refs], [leaf_ref[chip] for chip in range(leaf_ref.shape[0])])):
        total = parts[0].astype(f32)
        for part in parts[1:]:
            total += part.astype(f32)
        rows = pl.ds(i * TRUNK, TRUNK)
        buf[rows, :] = total.astype(bf16).T
        stores.append(pltpu.make_async_copy(buf.at[rows, :], out_ref.at[rows, :], sems.at[i]))
        stores[-1].start()
    for store in stores:
        store.wait()


def call(kernel, outs, in_specs, out_specs, scratch=(), flops=0, moved=0, aliases={}, limit=24):
    return pl.pallas_call(
        kernel,
        out_shape=outs,
        in_specs=in_specs,
        out_specs=out_specs,
        scratch_shapes=list(scratch),
        input_output_aliases=aliases,
        compiler_params=pltpu.CompilerParams(vmem_limit_bytes=limit * 1024 * 1024),
        cost_estimate=pl.CostEstimate(flops=flops, bytes_accessed=moved, transcendentals=0),
    )


def shards(queries, key_rows, value_rows, grad_out, w_key, w_value, trunk_len, leaf_len, leaf_tree):
    count = lax.axis_size("seg")
    heads = lax.axis_size("kvh")
    chips = heads // 2
    leaf_rows = LEAF * count
    row_width = queries.shape[1]
    hidden = w_key.shape[0]
    columns = hidden // heads
    out = jax.ShapeDtypeStruct
    dma = pltpu.SemaphoreType.DMA

    vm = pltpu.VMEM

    send = call(
        send_kernel,
        out((count * OUT_ROWS, HEAD), bf16),
        [hbm] * 5,
        hbm,
        [
            vm((count, count), jnp.int32),
            vm((leaf_rows, row_width), bf16),
            vm((leaf_rows, row_width), bf16),
            vm((leaf_rows, HEAD), bf16),
            vm((leaf_rows, HEAD), bf16),
            vm((count * OUT_ROWS, HEAD), f32),
            vm((count * OUT_ROWS, HEAD), bf16),
            dma((5,)),
            dma((2,)),
        ],
        flops=10**8,
        moved=10**6,
        limit=60,
    )(queries, grad_out, key_rows, value_rows, leaf_tree)
    got = lax.all_to_all(
        send.reshape(count, OUT_ROWS, HEAD), "seg", split_axis=0, concat_axis=0, tiled=True
    ).reshape(count * OUT_ROWS, HEAD)

    keys_all = TRUNK + leaf_rows
    dq, trunk_dkv, own, give = call(
        trunk_kernel,
        [
            out(queries.shape, bf16),
            out((TRUNK, 2 * HEAD), f32),
            out((2, chips, columns, HEAD), bf16),
            out((2, chips, columns, HEAD), bf16),
        ],
        [hbm] * 7,
        [hbm] * 2 + [vmem, hbm],
        [
            vm((TRUNK, row_width), bf16),
            vm((TRUNK, row_width), bf16),
            vm((TRUNK, HEAD), bf16),
            vm((TRUNK, HEAD), bf16),
            pltpu.SMEM((count,), jnp.int32),
            vm((GROUP * TRUNK, TRUNK), bf16),
            vm((GROUP * TRUNK, TRUNK), bf16),
            vm((TRUNK, row_width), bf16),
            vm((TRUNK, 2 * HEAD), f32),
            vm((2, chips, columns, HEAD), bf16),
            dma((5,)),
            dma((2,)),
            dma((2 * chips,)),
            dma((2 * chips,)),
            dma((2 * chips,)),
        ],
        flops=4 * 10**10,
        moved=10**7,
        limit=60,
    )(queries, grad_out, key_rows, value_rows, trunk_len, w_key, w_value)

    def swap(value):
        return lax.ppermute(value, "kvh", [(i, i ^ 1) for i in range(heads)])

    other = swap(give)

    back, leaf_dkv = call(
        leaf_kernel,
        [out((count * BACK_ROWS, HEAD), bf16), out((TRUNK, 2 * HEAD), f32)],
        [vmem] * 5 + [hbm],
        [hbm, vmem],
        [
            vm((count * OUT_ROWS, HEAD), f32),
            vm((count * BACK_ROWS, HEAD), f32),
            vm((GROUP * leaf_rows, HEAD), bf16),
            vm((GROUP * leaf_rows, HEAD), bf16),
            vm((GROUP * leaf_rows, keys_all), bf16),
            vm((GROUP * leaf_rows, keys_all), bf16),
            vm((count * BACK_ROWS, HEAD), bf16),
            pltpu.SMEM((count,), jnp.int32),
            dma,
            dma,
        ],
        flops=4 * 10**10,
        moved=10**6,
    )(got, key_rows, value_rows, leaf_tree, leaf_len, trunk_len)
    trunk_kv = (trunk_dkv + leaf_dkv).astype(bf16)

    part_flops = 2 * TRUNK * 4 * HEAD * chips * columns
    part_shape = (columns, TRUNK)
    steps = ((2, 1, 3), (2, 3, 1))
    *trunk_parts, token = call(
        functools.partial(trunk_part_kernel, steps),
        [out(part_shape, bf16)] * chips + [out((8, HEAD), f32)],
        [vmem] * 4,
        [hbm] * chips + [vmem],
        [vm((chips,) + part_shape, bf16), dma((chips,))],
        flops=part_flops,
        moved=4 * 10**6,
    )(trunk_kv, swap(trunk_kv), own, other)
    trunk_came = [trunk_parts[-1]]
    for i in range(chips - 1):
        route = [(2 * x + c, 2 * ((x + steps[c][i]) % chips) + c) for x in range(chips) for c in range(2)]
        trunk_came.append(lax.ppermute(trunk_parts[i], "kvh", route))
    back = lax.all_to_all(
        back.reshape(count, BACK_ROWS, HEAD), "seg", split_axis=0, concat_axis=0, tiled=True
    ).reshape(count * BACK_ROWS, HEAD)
    leaf_kv = call(
        leaf_kv_kernel,
        out((leaf_rows, 2 * HEAD), bf16),
        [vmem] * 2,
        vmem,
        [vm((count * BACK_ROWS, HEAD), f32)],
        flops=10**7,
        moved=10**6,
    )(back, token)
    grad_query, token = call(
        leaf_query_kernel,
        [out(queries.shape, bf16), out((8, HEAD), f32)],
        [vmem, hbm],
        [hbm, vmem],
        [vm((count * BACK_ROWS, HEAD), f32), vm((leaf_rows, row_width), bf16), dma],
        flops=10**8,
        moved=10**6,
        aliases={1: 0},
    )(back, dq)
    parts = call(
        leaf_part_kernel,
        out((chips, columns, leaf_rows), bf16),
        [vmem] * 5,
        vmem,
        flops=10**7,
        moved=4 * 10**6,
    )(leaf_kv, swap(leaf_kv), own, other, token)
    parts, *trunk_came = lax.optimization_barrier((parts, *trunk_came))
    came = lax.all_to_all(
        parts,
        "kvh",
        split_axis=0,
        concat_axis=0,
        tiled=True,
        axis_index_groups=[[2 * x + c for x in range(chips)] for c in range(2)],
    )
    grad_hidden = call(
        hidden_kernel,
        out((TRUNK + leaf_rows, columns), bf16),
        [vmem] * (1 + chips),
        hbm,
        [vm((TRUNK + leaf_rows, columns), bf16), dma((2,))],
        flops=10**6,
        moved=10**6,
    )(came, *trunk_came)
    return (grad_query, grad_hidden)


def solution(mesh):
    in_specs = (
        P("seg", "kvh"),
        P("seg", "kvh"),
        P("seg", "kvh"),
        P("seg", "kvh"),
        P(None, "kvh"),
        P(None, "kvh"),
        P(),
        P(),
        P(),
    )
    out_specs = (P("seg", "kvh"), P("seg", "kvh"))
    return jax.shard_map(shards, mesh=mesh, in_specs=in_specs, out_specs=out_specs, check_vma=False)
```

```python
import functools
import math

import jax
import jax.numpy as jnp
from jax import lax
from jax.experimental import pallas as pl
from jax.experimental.pallas import tpu as pltpu
from jax.sharding import PartitionSpec as P

GROUP = 5
TRUNK = 128
LEAF = 2
HEAD = 128
OUT_TILES = 2 * GROUP + 2
OUT_ROWS = OUT_TILES * LEAF
BACK_TILES = GROUP + 2
BACK_ROWS = 16
VERY_NEGATIVE = -1e30
SCALE = 1.0 / math.sqrt(HEAD)

f32 = jnp.float32
bf16 = jnp.bfloat16
vmem = pl.BlockSpec(memory_space=pltpu.VMEM)
smem = pl.BlockSpec(memory_space=pltpu.SMEM)
hbm = pl.BlockSpec(memory_space=pltpu.HBM)


def dot(a, b, contract):
    return lax.dot_general(a, b, ((contract[0:1], contract[1:2]), ((), ())), preferred_element_type=f32)


def leaf_selector(leaf_tree_ref, seg):
    count = leaf_tree_ref.shape[0]
    tree_row = leaf_tree_ref[pl.ds(seg, 1), :].astype(f32).astype(bf16)
    tree_rows = jnp.broadcast_to(tree_row, (16, count))
    leaf = lax.broadcasted_iota(jnp.int32, (count, LEAF * count), 0)
    col = lax.broadcasted_iota(jnp.int32, (count, LEAF * count), 1)
    repeat = (leaf == (col >> 1)).astype(f32).astype(bf16)
    tree_of_col = dot(tree_rows, repeat, (1, 0))[0:1, :].astype(jnp.int32)
    row = lax.broadcasted_iota(jnp.int32, (LEAF * count, LEAF * count), 0)
    col = lax.broadcasted_iota(jnp.int32, (LEAF * count, LEAF * count), 1)
    row_pos = (row >= count).astype(jnp.int32)
    hit = (tree_of_col == row - row_pos * count) & (row_pos == (col & 1))
    return hit.astype(f32).astype(bf16)


def copies(pairs, sems):
    started = [pltpu.make_async_copy(src, dst, sems.at[i]) for i, (src, dst) in enumerate(pairs)]
    for copy in started:
        copy.start()
    return started


def send_kernel(
    q_ref, g_ref, k_ref, v_ref, leaf_tree_ref,
    out_ref, tree_ref, q_buf, g_buf, k_buf, v_buf, rows_ref, out_buf, sems, out_sems,
):
    count = tree_ref.shape[0]
    leaves = pl.ds(TRUNK, LEAF * count)
    loads = [(leaf_tree_ref, tree_ref)]
    loads += [(src.at[leaves, :], dst) for src, dst in zip((q_ref, g_ref, k_ref, v_ref), (q_buf, g_buf, k_buf, v_buf))]
    loads = copies(loads, sems)
    seg = lax.axis_index("seg")
    loads[0].wait()
    selector = leaf_selector(tree_ref, seg)
    half = count // 2
    stores = []
    for part in range(2):
        at = part * half
        chosen = jnp.concatenate([selector[a * count + at : a * count + at + half, :] for a in range(LEAF)], axis=0)
        tile = 0
        for load, ref in zip(loads[1:], (q_buf, g_buf, k_buf, v_buf)):
            if part == 0:
                load.wait()
            moved = dot(chosen, ref[...], (1, 0))
            for column in range(0, ref.shape[1], HEAD):
                for a in range(LEAF):
                    rows_ref[pl.ds(at * OUT_ROWS + tile * LEAF + a, half, OUT_ROWS), :] = moved[
                        a * half : (a + 1) * half, column : column + HEAD
                    ]
                tile += 1
        rows = pl.ds(at * OUT_ROWS, half * OUT_ROWS)
        out_buf[rows, :] = rows_ref[rows, :].astype(bf16)
        stores.append(pltpu.make_async_copy(out_buf.at[rows, :], out_ref.at[rows, :], out_sems.at[part]))
        stores[-1].start()
    for store in stores:
        store.wait()


def softmax_grads(scores, prob_grad, visible):
    masked = jnp.where(visible, scores, VERY_NEGATIVE)
    row_max = jnp.max(masked, axis=-1, keepdims=True)
    weights = jnp.where(visible, jnp.exp(masked - row_max), 0.0)
    row_total = jnp.maximum(jnp.sum(weights, axis=-1, keepdims=True), 1.0)
    probability = weights * (1.0 / row_total)
    row_delta = jnp.sum(probability * prob_grad, axis=-1, keepdims=True)
    score_grad = (probability * (prob_grad - row_delta)).astype(bf16)
    return probability.astype(bf16), score_grad


def leaf_visible(leaf_tree_ref, leaf_len_ref, trunk_len, seg):
    count = leaf_tree_ref.shape[0]
    in_len = jnp.sum(jnp.where(leaf_tree_ref[...] == seg, leaf_len_ref[...], 0), axis=1, keepdims=True)
    row_len = jnp.concatenate([in_len] * LEAF, axis=0)
    leaf_rows = LEAF * count
    shape = (leaf_rows, TRUNK + leaf_rows)
    row = lax.broadcasted_iota(jnp.int32, shape, 0)
    col = lax.broadcasted_iota(jnp.int32, shape, 1)
    row_pos = (row >= count).astype(jnp.int32)
    leaf_col = col - TRUNK
    col_pos = (leaf_col >= count).astype(jnp.int32)
    own = (row - row_pos * count == leaf_col - col_pos * count) & (col_pos <= row_pos)
    visible = ((col < trunk_len) & (col < TRUNK)) | ((col >= TRUNK) & own)
    return visible & (row_pos < row_len)


def weight_pairs(w_key_ref, w_value_ref, to_ref, core):
    chips, block = to_ref.shape[1:3]
    pairs = []
    for chip in range(chips):
        rows = pl.ds(pl.multiple_of((2 * chip + core) * block, block), block)
        pairs += [(w.at[rows, :], to_ref.at[part, chip]) for part, w in enumerate((w_key_ref, w_value_ref))]
    return pairs


def trunk_kernel(
    q_in, g_in, k_in, v_in, trunk_len_in, w_key_ref, w_value_ref,
    dq_ref, dkv_ref, own_ref, give_ref,
    q_ref, g_ref, k_ref, v_ref, trunk_len_ref, ds_buf, p_buf, dq_buf, dkv_buf, give_buf,
    sems, out_sems, own_sems, give_sems, gave_sems,
):
    trunk = pl.ds(0, TRUNK)
    core = lax.axis_index("kvh") & 1
    chips = own_ref.shape[1]
    loads = copies(
        [
            (trunk_len_in, trunk_len_ref),
            (k_in.at[trunk, :], k_ref),
            (v_in.at[trunk, :], v_ref),
            (q_in.at[trunk, :], q_ref),
            (g_in.at[trunk, :], g_ref),
        ],
        sems,
    )
    give_loads = copies(weight_pairs(w_key_ref, w_value_ref, give_buf, 1 - core), give_sems)
    own_loads = copies(weight_pairs(w_key_ref, w_value_ref, own_ref, core), own_sems)
    for load in loads:
        load.wait()
    trunk_len = trunk_len_ref[lax.axis_index("seg")]
    keys = k_ref[...]
    values = v_ref[...]
    row = lax.broadcasted_iota(jnp.int32, (TRUNK, TRUNK), 0)
    col = lax.broadcasted_iota(jnp.int32, (TRUNK, TRUNK), 1)
    visible = (col <= row) & (row < trunk_len)
    stores = []
    for g in range(GROUP):
        columns = slice(g * HEAD, (g + 1) * HEAD)
        rows = slice(g * TRUNK, (g + 1) * TRUNK)
        scores = dot(q_ref[:, columns], keys, (1, 1)) * SCALE
        prob_grad = dot(g_ref[:, columns], values, (1, 1))
        p_buf[rows, :], ds_buf[rows, :] = softmax_grads(scores, prob_grad, visible)
        if g == 1:
            for i, load in enumerate(give_loads):
                load.wait()
                part, chip = i % 2, i // 2
                stores += copies([(give_buf.at[part, chip], give_ref.at[part, chip])], gave_sems.at[pl.ds(i, 1)])
    query_grad = dot(ds_buf[...], keys, (1, 0)) * SCALE
    for g in range(GROUP):
        dq_buf[:, g * HEAD : (g + 1) * HEAD] = query_grad[g * TRUNK : (g + 1) * TRUNK, :].astype(bf16)
    head_q = jnp.concatenate([q_ref[:, g * HEAD : (g + 1) * HEAD] for g in range(GROUP)], axis=0)
    head_g = jnp.concatenate([g_ref[:, g * HEAD : (g + 1) * HEAD] for g in range(GROUP)], axis=0)
    dkv_buf[:, 0:HEAD] = dot(ds_buf[...], head_q, (0, 0)) * SCALE
    dkv_buf[:, HEAD:] = dot(p_buf[...], head_g, (0, 0))
    stores += copies([(dq_buf, dq_ref.at[trunk, :]), (dkv_buf, dkv_ref)], out_sems)
    for copy in stores + own_loads:
        copy.wait()


def leaf_kernel(
    in_ref, k_ref, v_ref, leaf_tree_ref, leaf_len_ref, trunk_len_in,
    out_ref, dkv_ref, rows_ref, back_ref, q_buf, g_buf, ds_buf, p_buf, out_buf, trunk_len_ref, sem, out_sem,
):
    load = pltpu.make_async_copy(trunk_len_in, trunk_len_ref, sem)
    load.start()
    count = leaf_tree_ref.shape[0]
    leaf_rows = LEAF * count
    rows_ref[...] = in_ref[...].astype(f32)

    def gather(tile):
        parts = [rows_ref[pl.ds(tile * LEAF + a, count, OUT_ROWS), :] for a in range(LEAF)]
        return jnp.concatenate(parts, axis=0).astype(bf16)

    keys = jnp.concatenate([k_ref[0:TRUNK, :], gather(2 * GROUP)], axis=0)
    values = jnp.concatenate([v_ref[0:TRUNK, :], gather(2 * GROUP + 1)], axis=0)
    seg = lax.axis_index("seg")
    load.wait()
    visible = leaf_visible(leaf_tree_ref, leaf_len_ref, trunk_len_ref[seg], seg)
    for g in range(GROUP):
        rows = slice(g * leaf_rows, (g + 1) * leaf_rows)
        head_q = gather(g)
        head_g = gather(GROUP + g)
        q_buf[rows, :] = head_q
        g_buf[rows, :] = head_g
        scores = dot(head_q, keys, (1, 1)) * SCALE
        prob_grad = dot(head_g, values, (1, 1))
        p_buf[rows, :], ds_buf[rows, :] = softmax_grads(scores, prob_grad, visible)
    query_grad = dot(ds_buf[...], keys, (1, 0)) * SCALE
    for g in range(GROUP):
        for a in range(LEAF):
            at = g * leaf_rows + a * count
            back_ref[pl.ds(g * LEAF + a, count, BACK_ROWS), :] = query_grad[at : at + count, :]
    key_grad = dot(ds_buf[...], q_buf[...], (0, 0)) * SCALE
    value_grad = dot(p_buf[...], g_buf[...], (0, 0))
    for a in range(LEAF):
        at = TRUNK + a * count
        back_ref[pl.ds(GROUP * LEAF + a, count, BACK_ROWS), :] = key_grad[at : at + count, :]
        back_ref[pl.ds((GROUP + 1) * LEAF + a, count, BACK_ROWS), :] = value_grad[at : at + count, :]
    leaf = lax.broadcasted_iota(jnp.int32, (count, count), 1)
    number = jnp.sum(jnp.where(leaf_tree_ref[...] == seg, leaf, 0), axis=1, keepdims=True).astype(f32)
    for spare in range(BACK_TILES * LEAF, BACK_ROWS):
        back_ref[pl.ds(spare, count, BACK_ROWS), :] = jnp.broadcast_to(number, (count, HEAD))
    out_buf[...] = back_ref[...].astype(bf16)
    store = pltpu.make_async_copy(out_buf, out_ref, out_sem)
    store.start()
    dkv_ref[:, 0:HEAD] = key_grad[0:TRUNK, :]
    dkv_ref[:, HEAD:] = value_grad[0:TRUNK, :]
    store.wait()


def back_selector(rows_ref):
    count = rows_ref.shape[0] // BACK_ROWS
    number = rows_ref[pl.ds(BACK_TILES * LEAF, count, BACK_ROWS), :].astype(jnp.int32)
    col = lax.broadcasted_iota(jnp.int32, number.shape, 1)
    hits = [((number == (col >> 1)) & ((col & 1) == a)).astype(f32) for a in range(LEAF)]
    return jnp.concatenate(hits, axis=0)[:, 0 : LEAF * count].astype(bf16)


def moved_tile(rows_ref, selector, tile):
    count = rows_ref.shape[0] // BACK_ROWS
    parts = [rows_ref[pl.ds(tile * LEAF + a, count, BACK_ROWS), :] for a in range(LEAF)]
    return dot(selector, jnp.concatenate(parts, axis=0).astype(bf16), (0, 0)).astype(bf16)


def leaf_kv_kernel(in_ref, after_ref, out_ref, rows_ref):
    rows_ref[...] = in_ref[...].astype(f32)
    selector = back_selector(rows_ref)
    for part in range(2):
        out_ref[:, part * HEAD : (part + 1) * HEAD] = moved_tile(rows_ref, selector, GROUP + part)


def leaf_query_kernel(in_ref, dq_in_ref, dq_ref, token_ref, rows_ref, dq_buf, sem):
    rows_ref[...] = in_ref[...].astype(f32)
    selector = back_selector(rows_ref)
    for tile in range(GROUP):
        dq_buf[:, tile * HEAD : (tile + 1) * HEAD] = moved_tile(rows_ref, selector, tile)
    store = pltpu.make_async_copy(dq_buf, dq_ref.at[pl.ds(TRUNK, dq_buf.shape[0]), :], sem)
    store.start()
    token_ref[...] = jnp.zeros(token_ref.shape, f32)
    store.wait()


def chip_part(kv_ref, kv_other_ref, own_ref, other_ref, block):
    kv = jnp.concatenate([kv_ref[...], kv_other_ref[...]], axis=1)
    weight = jnp.concatenate([ref[part, block] for ref in (own_ref, other_ref) for part in range(2)], axis=1)
    return dot(weight, kv, (1, 1)).astype(bf16)


def trunk_part_kernel(steps, kv_ref, kv_other_ref, own_ref, other_ref, *refs):
    count = len(steps[0]) + 1
    chips = own_ref.shape[1]
    outs, token_ref, buf, sems = refs[:count], refs[count], refs[-2], refs[-1]
    kvh = lax.axis_index("kvh")
    chip, core = kvh >> 1, kvh & 1
    stores = []
    for i, (even, odd) in enumerate(zip(steps[0] + (0,), steps[1] + (0,))):
        block = lax.rem(chip + even + core * (odd - even), chips)
        buf[i] = chip_part(kv_ref, kv_other_ref, own_ref, other_ref, block)
        stores.append(pltpu.make_async_copy(buf.at[i], outs[i], sems.at[i]))
        stores[-1].start()
    token_ref[...] = jnp.zeros(token_ref.shape, f32)
    for store in stores:
        store.wait()


def leaf_part_kernel(kv_ref, kv_other_ref, own_ref, other_ref, after_ref, out_ref):
    for block in range(out_ref.shape[0]):
        out_ref[block] = chip_part(kv_ref, kv_other_ref, own_ref, other_ref, block)


def hidden_kernel(leaf_ref, *refs):
    trunk_refs, (out_ref, buf, sems) = refs[:-3], refs[-3:]
    stores = []
    for i, parts in enumerate(([ref[...] for ref in trunk_refs], [leaf_ref[chip] for chip in range(leaf_ref.shape[0])])):
        total = parts[0].astype(f32)
        for part in parts[1:]:
            total += part.astype(f32)
        rows = pl.ds(i * TRUNK, TRUNK)
        buf[rows, :] = total.astype(bf16).T
        stores.append(pltpu.make_async_copy(buf.at[rows, :], out_ref.at[rows, :], sems.at[i]))
        stores[-1].start()
    for store in stores:
        store.wait()


def call(kernel, outs, in_specs, out_specs, scratch=(), flops=0, moved=0, aliases={}, limit=24):
    return pl.pallas_call(
        kernel,
        out_shape=outs,
        in_specs=in_specs,
        out_specs=out_specs,
        scratch_shapes=list(scratch),
        input_output_aliases=aliases,
        compiler_params=pltpu.CompilerParams(vmem_limit_bytes=limit * 1024 * 1024),
        cost_estimate=pl.CostEstimate(flops=flops, bytes_accessed=moved, transcendentals=0),
    )


def shards(queries, key_rows, value_rows, grad_out, w_key, w_value, trunk_len, leaf_len, leaf_tree):
    count = lax.axis_size("seg")
    heads = lax.axis_size("kvh")
    chips = heads // 2
    leaf_rows = LEAF * count
    row_width = queries.shape[1]
    hidden = w_key.shape[0]
    columns = hidden // heads
    out = jax.ShapeDtypeStruct
    dma = pltpu.SemaphoreType.DMA

    vm = pltpu.VMEM

    send = call(
        send_kernel,
        out((count * OUT_ROWS, HEAD), bf16),
        [hbm] * 5,
        hbm,
        [
            vm((count, count), jnp.int32),
            vm((leaf_rows, row_width), bf16),
            vm((leaf_rows, row_width), bf16),
            vm((leaf_rows, HEAD), bf16),
            vm((leaf_rows, HEAD), bf16),
            vm((count * OUT_ROWS, HEAD), f32),
            vm((count * OUT_ROWS, HEAD), bf16),
            dma((5,)),
            dma((2,)),
        ],
        flops=10**8,
        moved=10**6,
        limit=60,
    )(queries, grad_out, key_rows, value_rows, leaf_tree)
    got = lax.all_to_all(
        send.reshape(count, OUT_ROWS, HEAD), "seg", split_axis=0, concat_axis=0, tiled=True
    ).reshape(count * OUT_ROWS, HEAD)

    keys_all = TRUNK + leaf_rows
    dq, trunk_dkv, own, give = call(
        trunk_kernel,
        [
            out(queries.shape, bf16),
            out((TRUNK, 2 * HEAD), f32),
            out((2, chips, columns, HEAD), bf16),
            out((2, chips, columns, HEAD), bf16),
        ],
        [hbm] * 7,
        [hbm] * 2 + [vmem, hbm],
        [
            vm((TRUNK, row_width), bf16),
            vm((TRUNK, row_width), bf16),
            vm((TRUNK, HEAD), bf16),
            vm((TRUNK, HEAD), bf16),
            pltpu.SMEM((count,), jnp.int32),
            vm((GROUP * TRUNK, TRUNK), bf16),
            vm((GROUP * TRUNK, TRUNK), bf16),
            vm((TRUNK, row_width), bf16),
            vm((TRUNK, 2 * HEAD), f32),
            vm((2, chips, columns, HEAD), bf16),
            dma((5,)),
            dma((2,)),
            dma((2 * chips,)),
            dma((2 * chips,)),
            dma((2 * chips,)),
        ],
        flops=4 * 10**10,
        moved=10**7,
        limit=60,
    )(queries, grad_out, key_rows, value_rows, trunk_len, w_key, w_value)

    def swap(value):
        return lax.ppermute(value, "kvh", [(i, i ^ 1) for i in range(heads)])

    other = swap(give)

    back, leaf_dkv = call(
        leaf_kernel,
        [out((count * BACK_ROWS, HEAD), bf16), out((TRUNK, 2 * HEAD), f32)],
        [vmem] * 5 + [hbm],
        [hbm, vmem],
        [
            vm((count * OUT_ROWS, HEAD), f32),
            vm((count * BACK_ROWS, HEAD), f32),
            vm((GROUP * leaf_rows, HEAD), bf16),
            vm((GROUP * leaf_rows, HEAD), bf16),
            vm((GROUP * leaf_rows, keys_all), bf16),
            vm((GROUP * leaf_rows, keys_all), bf16),
            vm((count * BACK_ROWS, HEAD), bf16),
            pltpu.SMEM((count,), jnp.int32),
            dma,
            dma,
        ],
        flops=4 * 10**10,
        moved=10**6,
    )(got, key_rows, value_rows, leaf_tree, leaf_len, trunk_len)
    trunk_kv = (trunk_dkv + leaf_dkv).astype(bf16)

    part_flops = 2 * TRUNK * 4 * HEAD * chips * columns
    part_shape = (columns, TRUNK)
    steps = ((1, 3, 2), (1, 3, 2))
    *trunk_parts, token = call(
        functools.partial(trunk_part_kernel, steps),
        [out(part_shape, bf16)] * chips + [out((8, HEAD), f32)],
        [vmem] * 4,
        [hbm] * chips + [vmem],
        [vm((chips,) + part_shape, bf16), dma((chips,))],
        flops=part_flops,
        moved=4 * 10**6,
    )(trunk_kv, swap(trunk_kv), own, other)
    trunk_came = [trunk_parts[-1]]
    for i in range(chips - 1):
        route = [(2 * x + c, 2 * ((x + steps[c][i]) % chips) + c) for x in range(chips) for c in range(2)]
        trunk_came.append(lax.ppermute(trunk_parts[i], "kvh", route))
    back = lax.all_to_all(
        back.reshape(count, BACK_ROWS, HEAD), "seg", split_axis=0, concat_axis=0, tiled=True
    ).reshape(count * BACK_ROWS, HEAD)
    leaf_kv = call(
        leaf_kv_kernel,
        out((leaf_rows, 2 * HEAD), bf16),
        [vmem] * 2,
        vmem,
        [vm((count * BACK_ROWS, HEAD), f32)],
        flops=10**7,
        moved=10**6,
    )(back, token)
    grad_query, token = call(
        leaf_query_kernel,
        [out(queries.shape, bf16), out((8, HEAD), f32)],
        [vmem, hbm],
        [hbm, vmem],
        [vm((count * BACK_ROWS, HEAD), f32), vm((leaf_rows, row_width), bf16), dma],
        flops=10**8,
        moved=10**6,
        aliases={1: 0},
    )(back, dq)
    parts = call(
        leaf_part_kernel,
        out((chips, columns, leaf_rows), bf16),
        [vmem] * 5,
        vmem,
        flops=10**7,
        moved=4 * 10**6,
    )(leaf_kv, swap(leaf_kv), own, other, token)
    parts, *trunk_came = lax.optimization_barrier((parts, *trunk_came))
    came = lax.all_to_all(
        parts,
        "kvh",
        split_axis=0,
        concat_axis=0,
        tiled=True,
        axis_index_groups=[[2 * x + c for x in range(chips)] for c in range(2)],
    )
    grad_hidden = call(
        hidden_kernel,
        out((TRUNK + leaf_rows, columns), bf16),
        [vmem] * (1 + chips),
        hbm,
        [vm((TRUNK + leaf_rows, columns), bf16), dma((2,))],
        flops=10**6,
        moved=10**6,
    )(came, *trunk_came)
    return (grad_query, grad_hidden)


def solution(mesh):
    in_specs = (
        P("seg", "kvh"),
        P("seg", "kvh"),
        P("seg", "kvh"),
        P("seg", "kvh"),
        P(None, "kvh"),
        P(None, "kvh"),
        P(),
        P(),
        P(),
    )
    out_specs = (P("seg", "kvh"), P("seg", "kvh"))
    return jax.shard_map(shards, mesh=mesh, in_specs=in_specs, out_specs=out_specs, check_vma=False)
```

```python
import functools
import math

import jax
import jax.numpy as jnp
from jax import lax
from jax.experimental import pallas as pl
from jax.experimental.pallas import tpu as pltpu
from jax.sharding import PartitionSpec as P

GROUP = 5
TRUNK = 128
LEAF = 2
HEAD = 128
OUT_TILES = 2 * GROUP + 2
OUT_ROWS = OUT_TILES * LEAF
BACK_TILES = GROUP + 2
BACK_ROWS = 16
VERY_NEGATIVE = -1e30
SCALE = 1.0 / math.sqrt(HEAD)

f32 = jnp.float32
bf16 = jnp.bfloat16
vmem = pl.BlockSpec(memory_space=pltpu.VMEM)
smem = pl.BlockSpec(memory_space=pltpu.SMEM)
hbm = pl.BlockSpec(memory_space=pltpu.HBM)


def dot(a, b, contract):
    return lax.dot_general(a, b, ((contract[0:1], contract[1:2]), ((), ())), preferred_element_type=f32)


def leaf_selector(leaf_tree_ref, seg):
    count = leaf_tree_ref.shape[0]
    tree_row = leaf_tree_ref[pl.ds(seg, 1), :].astype(f32).astype(bf16)
    tree_rows = jnp.broadcast_to(tree_row, (16, count))
    leaf = lax.broadcasted_iota(jnp.int32, (count, LEAF * count), 0)
    col = lax.broadcasted_iota(jnp.int32, (count, LEAF * count), 1)
    repeat = (leaf == (col >> 1)).astype(f32).astype(bf16)
    tree_of_col = dot(tree_rows, repeat, (1, 0))[0:1, :].astype(jnp.int32)
    row = lax.broadcasted_iota(jnp.int32, (LEAF * count, LEAF * count), 0)
    col = lax.broadcasted_iota(jnp.int32, (LEAF * count, LEAF * count), 1)
    row_pos = (row >= count).astype(jnp.int32)
    hit = (tree_of_col == row - row_pos * count) & (row_pos == (col & 1))
    return hit.astype(f32).astype(bf16)


def copies(pairs, sems):
    started = [pltpu.make_async_copy(src, dst, sems.at[i]) for i, (src, dst) in enumerate(pairs)]
    for copy in started:
        copy.start()
    return started


def send_kernel(
    q_ref, g_ref, k_ref, v_ref, leaf_tree_ref,
    out_ref, tree_ref, q_buf, g_buf, k_buf, v_buf, rows_ref, out_buf, sems, out_sems,
):
    count = tree_ref.shape[0]
    leaves = pl.ds(TRUNK, LEAF * count)
    loads = [(leaf_tree_ref, tree_ref)]
    loads += [(src.at[leaves, :], dst) for src, dst in zip((q_ref, g_ref, k_ref, v_ref), (q_buf, g_buf, k_buf, v_buf))]
    loads = copies(loads, sems)
    seg = lax.axis_index("seg")
    loads[0].wait()
    selector = leaf_selector(tree_ref, seg)
    half = count // 4
    stores = []
    for part in range(4):
        at = part * half
        chosen = jnp.concatenate([selector[a * count + at : a * count + at + half, :] for a in range(LEAF)], axis=0)
        tile = 0
        for load, ref in zip(loads[1:], (q_buf, g_buf, k_buf, v_buf)):
            if part == 0:
                load.wait()
            moved = dot(chosen, ref[...], (1, 0))
            for column in range(0, ref.shape[1], HEAD):
                for a in range(LEAF):
                    rows_ref[pl.ds(at * OUT_ROWS + tile * LEAF + a, half, OUT_ROWS), :] = moved[
                        a * half : (a + 1) * half, column : column + HEAD
                    ]
                tile += 1
        rows = pl.ds(at * OUT_ROWS, half * OUT_ROWS)
        out_buf[rows, :] = rows_ref[rows, :].astype(bf16)
        stores.append(pltpu.make_async_copy(out_buf.at[rows, :], out_ref.at[rows, :], out_sems.at[part]))
        stores[-1].start()
    for store in stores:
        store.wait()


def softmax_grads(scores, prob_grad, visible):
    masked = jnp.where(visible, scores, VERY_NEGATIVE)
    row_max = jnp.max(masked, axis=-1, keepdims=True)
    weights = jnp.where(visible, jnp.exp(masked - row_max), 0.0)
    row_total = jnp.maximum(jnp.sum(weights, axis=-1, keepdims=True), 1.0)
    probability = weights * (1.0 / row_total)
    row_delta = jnp.sum(probability * prob_grad, axis=-1, keepdims=True)
    score_grad = (probability * (prob_grad - row_delta)).astype(bf16)
    return probability.astype(bf16), score_grad


def leaf_visible(leaf_tree_ref, leaf_len_ref, trunk_len, seg):
    count = leaf_tree_ref.shape[0]
    in_len = jnp.sum(jnp.where(leaf_tree_ref[...] == seg, leaf_len_ref[...], 0), axis=1, keepdims=True)
    row_len = jnp.concatenate([in_len] * LEAF, axis=0)
    leaf_rows = LEAF * count
    shape = (leaf_rows, TRUNK + leaf_rows)
    row = lax.broadcasted_iota(jnp.int32, shape, 0)
    col = lax.broadcasted_iota(jnp.int32, shape, 1)
    row_pos = (row >= count).astype(jnp.int32)
    leaf_col = col - TRUNK
    col_pos = (leaf_col >= count).astype(jnp.int32)
    own = (row - row_pos * count == leaf_col - col_pos * count) & (col_pos <= row_pos)
    visible = ((col < trunk_len) & (col < TRUNK)) | ((col >= TRUNK) & own)
    return visible & (row_pos < row_len)


def weight_pairs(w_key_ref, w_value_ref, to_ref, core):
    chips, block = to_ref.shape[1:3]
    pairs = []
    for chip in range(chips):
        rows = pl.ds(pl.multiple_of((2 * chip + core) * block, block), block)
        pairs += [(w.at[rows, :], to_ref.at[part, chip]) for part, w in enumerate((w_key_ref, w_value_ref))]
    return pairs


def trunk_kernel(
    q_in, g_in, k_in, v_in, trunk_len_in, w_key_ref, w_value_ref,
    dq_ref, dkv_ref, own_ref, give_ref,
    q_ref, g_ref, k_ref, v_ref, trunk_len_ref, ds_buf, p_buf, dq_buf, dkv_buf, give_buf,
    sems, out_sems, own_sems, give_sems, gave_sems,
):
    trunk = pl.ds(0, TRUNK)
    core = lax.axis_index("kvh") & 1
    chips = own_ref.shape[1]
    loads = copies(
        [
            (trunk_len_in, trunk_len_ref),
            (k_in.at[trunk, :], k_ref),
            (v_in.at[trunk, :], v_ref),
            (q_in.at[trunk, :], q_ref),
            (g_in.at[trunk, :], g_ref),
        ],
        sems,
    )
    give_loads = copies(weight_pairs(w_key_ref, w_value_ref, give_buf, 1 - core), give_sems)
    own_loads = copies(weight_pairs(w_key_ref, w_value_ref, own_ref, core), own_sems)
    for load in loads:
        load.wait()
    trunk_len = trunk_len_ref[lax.axis_index("seg")]
    keys = k_ref[...]
    values = v_ref[...]
    row = lax.broadcasted_iota(jnp.int32, (TRUNK, TRUNK), 0)
    col = lax.broadcasted_iota(jnp.int32, (TRUNK, TRUNK), 1)
    visible = (col <= row) & (row < trunk_len)
    stores = []
    for g in range(GROUP):
        columns = slice(g * HEAD, (g + 1) * HEAD)
        rows = slice(g * TRUNK, (g + 1) * TRUNK)
        scores = dot(q_ref[:, columns], keys, (1, 1)) * SCALE
        prob_grad = dot(g_ref[:, columns], values, (1, 1))
        p_buf[rows, :], ds_buf[rows, :] = softmax_grads(scores, prob_grad, visible)
        if g == 1:
            for i, load in enumerate(give_loads):
                load.wait()
                part, chip = i % 2, i // 2
                stores += copies([(give_buf.at[part, chip], give_ref.at[part, chip])], gave_sems.at[pl.ds(i, 1)])
    query_grad = dot(ds_buf[...], keys, (1, 0)) * SCALE
    for g in range(GROUP):
        dq_buf[:, g * HEAD : (g + 1) * HEAD] = query_grad[g * TRUNK : (g + 1) * TRUNK, :].astype(bf16)
    head_q = jnp.concatenate([q_ref[:, g * HEAD : (g + 1) * HEAD] for g in range(GROUP)], axis=0)
    head_g = jnp.concatenate([g_ref[:, g * HEAD : (g + 1) * HEAD] for g in range(GROUP)], axis=0)
    dkv_buf[:, 0:HEAD] = dot(ds_buf[...], head_q, (0, 0)) * SCALE
    dkv_buf[:, HEAD:] = dot(p_buf[...], head_g, (0, 0))
    stores += copies([(dq_buf, dq_ref.at[trunk, :]), (dkv_buf, dkv_ref)], out_sems)
    for copy in stores + own_loads:
        copy.wait()


def leaf_kernel(
    in_ref, k_ref, v_ref, leaf_tree_ref, leaf_len_ref, trunk_len_in,
    out_ref, dkv_ref, rows_ref, back_ref, q_buf, g_buf, ds_buf, p_buf, out_buf, trunk_len_ref, sem, out_sems,
):
    load = pltpu.make_async_copy(trunk_len_in, trunk_len_ref, sem)
    load.start()
    count = leaf_tree_ref.shape[0]
    leaf_rows = LEAF * count
    rows_ref[...] = in_ref[...].astype(f32)

    def gather(tile):
        parts = [rows_ref[pl.ds(tile * LEAF + a, count, OUT_ROWS), :] for a in range(LEAF)]
        return jnp.concatenate(parts, axis=0).astype(bf16)

    keys = jnp.concatenate([k_ref[0:TRUNK, :], gather(2 * GROUP)], axis=0)
    values = jnp.concatenate([v_ref[0:TRUNK, :], gather(2 * GROUP + 1)], axis=0)
    seg = lax.axis_index("seg")
    load.wait()
    visible = leaf_visible(leaf_tree_ref, leaf_len_ref, trunk_len_ref[seg], seg)
    for g in range(GROUP):
        rows = slice(g * leaf_rows, (g + 1) * leaf_rows)
        head_q = gather(g)
        head_g = gather(GROUP + g)
        q_buf[rows, :] = head_q
        g_buf[rows, :] = head_g
        scores = dot(head_q, keys, (1, 1)) * SCALE
        prob_grad = dot(head_g, values, (1, 1))
        p_buf[rows, :], ds_buf[rows, :] = softmax_grads(scores, prob_grad, visible)
    query_grad = dot(ds_buf[...], keys, (1, 0)) * SCALE
    for g in range(GROUP):
        for a in range(LEAF):
            at = g * leaf_rows + a * count
            back_ref[pl.ds(g * LEAF + a, count, BACK_ROWS), :] = query_grad[at : at + count, :]
    key_grad = dot(ds_buf[...], q_buf[...], (0, 0)) * SCALE
    value_grad = dot(p_buf[...], g_buf[...], (0, 0))
    for a in range(LEAF):
        at = TRUNK + a * count
        back_ref[pl.ds(GROUP * LEAF + a, count, BACK_ROWS), :] = key_grad[at : at + count, :]
        back_ref[pl.ds((GROUP + 1) * LEAF + a, count, BACK_ROWS), :] = value_grad[at : at + count, :]
    leaf = lax.broadcasted_iota(jnp.int32, (count, count), 1)
    number = jnp.sum(jnp.where(leaf_tree_ref[...] == seg, leaf, 0), axis=1, keepdims=True).astype(f32)
    for spare in range(BACK_TILES * LEAF, BACK_ROWS):
        back_ref[pl.ds(spare, count, BACK_ROWS), :] = jnp.broadcast_to(number, (count, HEAD))
    stores = []
    for part in range(4):
        rows = pl.ds(part * (count // 4) * BACK_ROWS, count // 4 * BACK_ROWS)
        out_buf[rows, :] = back_ref[rows, :].astype(bf16)
        stores += copies([(out_buf.at[rows, :], out_ref.at[rows, :])], out_sems.at[pl.ds(part, 1)])
    dkv_ref[:, 0:HEAD] = key_grad[0:TRUNK, :]
    dkv_ref[:, HEAD:] = value_grad[0:TRUNK, :]
    for store in stores:
        store.wait()


def back_selector(rows_ref):
    count = rows_ref.shape[0] // BACK_ROWS
    number = rows_ref[pl.ds(BACK_TILES * LEAF, count, BACK_ROWS), :].astype(jnp.int32)
    col = lax.broadcasted_iota(jnp.int32, number.shape, 1)
    hits = [((number == (col >> 1)) & ((col & 1) == a)).astype(f32) for a in range(LEAF)]
    return jnp.concatenate(hits, axis=0)[:, 0 : LEAF * count].astype(bf16)


def moved_tile(rows_ref, selector, tile):
    count = rows_ref.shape[0] // BACK_ROWS
    parts = [rows_ref[pl.ds(tile * LEAF + a, count, BACK_ROWS), :] for a in range(LEAF)]
    return dot(selector, jnp.concatenate(parts, axis=0).astype(bf16), (0, 0)).astype(bf16)


def leaf_kv_kernel(in_ref, after_ref, out_ref, rows_ref):
    rows_ref[...] = in_ref[...].astype(f32)
    selector = back_selector(rows_ref)
    for part in range(2):
        out_ref[:, part * HEAD : (part + 1) * HEAD] = moved_tile(rows_ref, selector, GROUP + part)


def leaf_query_kernel(in_ref, dq_in_ref, dq_ref, token_ref, rows_ref, dq_buf, sem):
    rows_ref[...] = in_ref[...].astype(f32)
    selector = back_selector(rows_ref)
    for tile in range(GROUP):
        dq_buf[:, tile * HEAD : (tile + 1) * HEAD] = moved_tile(rows_ref, selector, tile)
    store = pltpu.make_async_copy(dq_buf, dq_ref.at[pl.ds(TRUNK, dq_buf.shape[0]), :], sem)
    store.start()
    token_ref[...] = jnp.zeros(token_ref.shape, f32)
    store.wait()


def chip_part(kv_ref, kv_other_ref, own_ref, other_ref, block):
    kv = jnp.concatenate([kv_ref[...], kv_other_ref[...]], axis=1)
    weight = jnp.concatenate([ref[part, block] for ref in (own_ref, other_ref) for part in range(2)], axis=1)
    return dot(weight, kv, (1, 1)).astype(bf16)


def trunk_part_kernel(steps, kv_ref, kv_other_ref, own_ref, other_ref, *refs):
    count = len(steps[0]) + 1
    chips = own_ref.shape[1]
    outs, token_ref, buf, sems = refs[:count], refs[count], refs[-2], refs[-1]
    kvh = lax.axis_index("kvh")
    chip, core = kvh >> 1, kvh & 1
    stores = []
    for i, (even, odd) in enumerate(zip(steps[0] + (0,), steps[1] + (0,))):
        block = lax.rem(chip + even + core * (odd - even), chips)
        part = chip_part(kv_ref, kv_other_ref, own_ref, other_ref, block)
        if i == count - 1:
            outs[i][...] = part
        else:
            buf[i] = part
            stores.append(pltpu.make_async_copy(buf.at[i], outs[i], sems.at[i]))
            stores[-1].start()
    token_ref[...] = jnp.zeros(token_ref.shape, f32)
    for store in stores:
        store.wait()


def leaf_part_kernel(kv_ref, kv_other_ref, own_ref, other_ref, after_ref, out_ref):
    for block in range(out_ref.shape[0]):
        out_ref[block] = chip_part(kv_ref, kv_other_ref, own_ref, other_ref, block)


def hidden_kernel(leaf_ref, *refs):
    trunk_refs, (out_ref, buf, sems) = refs[:-3], refs[-3:]
    stores = []
    for i, parts in enumerate(([ref[...] for ref in trunk_refs], [leaf_ref[chip] for chip in range(leaf_ref.shape[0])])):
        total = parts[0].astype(f32)
        for part in parts[1:]:
            total += part.astype(f32)
        rows = pl.ds(i * TRUNK, TRUNK)
        buf[rows, :] = total.astype(bf16).T
        stores.append(pltpu.make_async_copy(buf.at[rows, :], out_ref.at[rows, :], sems.at[i]))
        stores[-1].start()
    for store in stores:
        store.wait()


def call(kernel, outs, in_specs, out_specs, scratch=(), flops=0, moved=0, aliases={}, limit=24):
    return pl.pallas_call(
        kernel,
        out_shape=outs,
        in_specs=in_specs,
        out_specs=out_specs,
        scratch_shapes=list(scratch),
        input_output_aliases=aliases,
        compiler_params=pltpu.CompilerParams(vmem_limit_bytes=limit * 1024 * 1024),
        cost_estimate=pl.CostEstimate(flops=flops, bytes_accessed=moved, transcendentals=0),
    )


def shards(queries, key_rows, value_rows, grad_out, w_key, w_value, trunk_len, leaf_len, leaf_tree):
    count = lax.axis_size("seg")
    heads = lax.axis_size("kvh")
    chips = heads // 2
    leaf_rows = LEAF * count
    row_width = queries.shape[1]
    hidden = w_key.shape[0]
    columns = hidden // heads
    out = jax.ShapeDtypeStruct
    dma = pltpu.SemaphoreType.DMA

    vm = pltpu.VMEM

    send = call(
        send_kernel,
        out((count * OUT_ROWS, HEAD), bf16),
        [hbm] * 5,
        hbm,
        [
            vm((count, count), jnp.int32),
            vm((leaf_rows, row_width), bf16),
            vm((leaf_rows, row_width), bf16),
            vm((leaf_rows, HEAD), bf16),
            vm((leaf_rows, HEAD), bf16),
            vm((count * OUT_ROWS, HEAD), f32),
            vm((count * OUT_ROWS, HEAD), bf16),
            dma((5,)),
            dma((4,)),
        ],
        flops=10**8,
        moved=10**6,
        limit=60,
    )(queries, grad_out, key_rows, value_rows, leaf_tree)
    got = lax.all_to_all(
        send.reshape(count, OUT_ROWS, HEAD), "seg", split_axis=0, concat_axis=0, tiled=True
    ).reshape(count * OUT_ROWS, HEAD)

    keys_all = TRUNK + leaf_rows
    dq, trunk_dkv, own, give = call(
        trunk_kernel,
        [
            out(queries.shape, bf16),
            out((TRUNK, 2 * HEAD), f32),
            out((2, chips, columns, HEAD), bf16),
            out((2, chips, columns, HEAD), bf16),
        ],
        [hbm] * 7,
        [hbm] * 2 + [vmem, hbm],
        [
            vm((TRUNK, row_width), bf16),
            vm((TRUNK, row_width), bf16),
            vm((TRUNK, HEAD), bf16),
            vm((TRUNK, HEAD), bf16),
            pltpu.SMEM((count,), jnp.int32),
            vm((GROUP * TRUNK, TRUNK), bf16),
            vm((GROUP * TRUNK, TRUNK), bf16),
            vm((TRUNK, row_width), bf16),
            vm((TRUNK, 2 * HEAD), f32),
            vm((2, chips, columns, HEAD), bf16),
            dma((5,)),
            dma((2,)),
            dma((2 * chips,)),
            dma((2 * chips,)),
            dma((2 * chips,)),
        ],
        flops=4 * 10**10,
        moved=10**7,
        limit=60,
    )(queries, grad_out, key_rows, value_rows, trunk_len, w_key, w_value)

    def swap(value):
        return lax.ppermute(value, "kvh", [(i, i ^ 1) for i in range(heads)])

    other = swap(give)

    back, leaf_dkv = call(
        leaf_kernel,
        [out((count * BACK_ROWS, HEAD), bf16), out((TRUNK, 2 * HEAD), f32)],
        [vmem] * 5 + [hbm],
        [hbm, vmem],
        [
            vm((count * OUT_ROWS, HEAD), f32),
            vm((count * BACK_ROWS, HEAD), f32),
            vm((GROUP * leaf_rows, HEAD), bf16),
            vm((GROUP * leaf_rows, HEAD), bf16),
            vm((GROUP * leaf_rows, keys_all), bf16),
            vm((GROUP * leaf_rows, keys_all), bf16),
            vm((count * BACK_ROWS, HEAD), bf16),
            pltpu.SMEM((count,), jnp.int32),
            dma,
            dma((4,)),
        ],
        flops=4 * 10**10,
        moved=10**6,
    )(got, key_rows, value_rows, leaf_tree, leaf_len, trunk_len)
    trunk_kv = (trunk_dkv + leaf_dkv).astype(bf16)

    part_flops = 2 * TRUNK * 4 * HEAD * chips * columns
    part_shape = (columns, TRUNK)
    steps = ((1, 3, 2), (1, 3, 2))
    *trunk_parts, token = call(
        functools.partial(trunk_part_kernel, steps),
        [out(part_shape, bf16)] * chips + [out((8, HEAD), f32)],
        [vmem] * 4,
        [hbm] * (chips - 1) + [vmem] * 2,
        [vm((chips - 1,) + part_shape, bf16), dma((chips - 1,))],
        flops=part_flops,
        moved=4 * 10**6,
    )(trunk_kv, swap(trunk_kv), own, other)
    trunk_came = [trunk_parts[-1]]
    for i in range(chips - 1):
        route = [(2 * x + c, 2 * ((x + steps[c][i]) % chips) + c) for x in range(chips) for c in range(2)]
        trunk_came.append(lax.ppermute(trunk_parts[i], "kvh", route))
    back = lax.all_to_all(
        back.reshape(count, BACK_ROWS, HEAD), "seg", split_axis=0, concat_axis=0, tiled=True
    ).reshape(count * BACK_ROWS, HEAD)
    leaf_kv = call(
        leaf_kv_kernel,
        out((leaf_rows, 2 * HEAD), bf16),
        [vmem] * 2,
        vmem,
        [vm((count * BACK_ROWS, HEAD), f32)],
        flops=10**7,
        moved=10**6,
    )(back, token)
    grad_query, token = call(
        leaf_query_kernel,
        [out(queries.shape, bf16), out((8, HEAD), f32)],
        [vmem, hbm],
        [hbm, vmem],
        [vm((count * BACK_ROWS, HEAD), f32), vm((leaf_rows, row_width), bf16), dma],
        flops=10**8,
        moved=10**6,
        aliases={1: 0},
    )(back, dq)
    parts = call(
        leaf_part_kernel,
        out((chips, columns, leaf_rows), bf16),
        [vmem] * 5,
        vmem,
        flops=10**7,
        moved=4 * 10**6,
    )(leaf_kv, swap(leaf_kv), own, other, token)
    parts, *trunk_came = lax.optimization_barrier((parts, *trunk_came))
    came = lax.all_to_all(
        parts,
        "kvh",
        split_axis=0,
        concat_axis=0,
        tiled=True,
        axis_index_groups=[[2 * x + c for x in range(chips)] for c in range(2)],
    )
    grad_hidden = call(
        hidden_kernel,
        out((TRUNK + leaf_rows, columns), bf16),
        [vmem] * (1 + chips),
        hbm,
        [vm((TRUNK + leaf_rows, columns), bf16), dma((2,))],
        flops=10**6,
        moved=10**6,
    )(came, *trunk_came)
    return (grad_query, grad_hidden)


def solution(mesh):
    in_specs = (
        P("seg", "kvh"),
        P("seg", "kvh"),
        P("seg", "kvh"),
        P("seg", "kvh"),
        P(None, "kvh"),
        P(None, "kvh"),
        P(),
        P(),
        P(),
    )
    out_specs = (P("seg", "kvh"), P("seg", "kvh"))
    return jax.shard_map(shards, mesh=mesh, in_specs=in_specs, out_specs=out_specs, check_vma=False)
```

```python
import functools
import math

import jax
import jax.numpy as jnp
from jax import lax
from jax.experimental import pallas as pl
from jax.experimental.pallas import tpu as pltpu
from jax.sharding import PartitionSpec as P

GROUP = 5
TRUNK = 128
LEAF = 2
HEAD = 128
OUT_TILES = 2 * GROUP + 2
OUT_ROWS = OUT_TILES * LEAF
BACK_TILES = GROUP + 2
BACK_ROWS = 16
VERY_NEGATIVE = -1e30
SCALE = 1.0 / math.sqrt(HEAD)

f32 = jnp.float32
bf16 = jnp.bfloat16
vmem = pl.BlockSpec(memory_space=pltpu.VMEM)
smem = pl.BlockSpec(memory_space=pltpu.SMEM)
hbm = pl.BlockSpec(memory_space=pltpu.HBM)


def dot(a, b, contract):
    return lax.dot_general(a, b, ((contract[0:1], contract[1:2]), ((), ())), preferred_element_type=f32)


def leaf_selector(leaf_tree_ref, seg):
    count = leaf_tree_ref.shape[0]
    tree_row = leaf_tree_ref[pl.ds(seg, 1), :].astype(f32).astype(bf16)
    tree_rows = jnp.broadcast_to(tree_row, (16, count))
    leaf = lax.broadcasted_iota(jnp.int32, (count, LEAF * count), 0)
    col = lax.broadcasted_iota(jnp.int32, (count, LEAF * count), 1)
    repeat = (leaf == (col >> 1)).astype(f32).astype(bf16)
    tree_of_col = dot(tree_rows, repeat, (1, 0))[0:1, :].astype(jnp.int32)
    row = lax.broadcasted_iota(jnp.int32, (LEAF * count, LEAF * count), 0)
    col = lax.broadcasted_iota(jnp.int32, (LEAF * count, LEAF * count), 1)
    row_pos = (row >= count).astype(jnp.int32)
    hit = (tree_of_col == row - row_pos * count) & (row_pos == (col & 1))
    return hit.astype(f32).astype(bf16)


def copies(pairs, sems):
    started = [pltpu.make_async_copy(src, dst, sems.at[i]) for i, (src, dst) in enumerate(pairs)]
    for copy in started:
        copy.start()
    return started


def send_kernel(
    q_ref, g_ref, k_ref, v_ref, leaf_tree_ref,
    out_ref, tree_ref, q_buf, g_buf, k_buf, v_buf, rows_ref, out_buf, sems, out_sems,
):
    count = tree_ref.shape[0]
    leaves = pl.ds(TRUNK, LEAF * count)
    loads = [(leaf_tree_ref, tree_ref)]
    loads += [(src.at[leaves, :], dst) for src, dst in zip((q_ref, g_ref, k_ref, v_ref), (q_buf, g_buf, k_buf, v_buf))]
    loads = copies(loads, sems)
    seg = lax.axis_index("seg")
    loads[0].wait()
    selector = leaf_selector(tree_ref, seg)
    half = count // 4
    stores = []
    for part in range(4):
        at = part * half
        chosen = jnp.concatenate([selector[a * count + at : a * count + at + half, :] for a in range(LEAF)], axis=0)
        tile = 0
        for load, ref in zip(loads[1:], (q_buf, g_buf, k_buf, v_buf)):
            if part == 0:
                load.wait()
            moved = dot(chosen, ref[...], (1, 0))
            for column in range(0, ref.shape[1], HEAD):
                for a in range(LEAF):
                    rows_ref[pl.ds(at * OUT_ROWS + tile * LEAF + a, half, OUT_ROWS), :] = moved[
                        a * half : (a + 1) * half, column : column + HEAD
                    ]
                tile += 1
        rows = pl.ds(at * OUT_ROWS, half * OUT_ROWS)
        out_buf[rows, :] = rows_ref[rows, :].astype(bf16)
        stores.append(pltpu.make_async_copy(out_buf.at[rows, :], out_ref.at[rows, :], out_sems.at[part]))
        stores[-1].start()
    for store in stores:
        store.wait()


def softmax_grads(scores, prob_grad, visible):
    masked = jnp.where(visible, scores, VERY_NEGATIVE)
    row_max = jnp.max(masked, axis=-1, keepdims=True)
    weights = jnp.where(visible, jnp.exp(masked - row_max), 0.0)
    row_total = jnp.maximum(jnp.sum(weights, axis=-1, keepdims=True), 1.0)
    probability = weights * (1.0 / row_total)
    row_delta = jnp.sum(probability * prob_grad, axis=-1, keepdims=True)
    score_grad = (probability * (prob_grad - row_delta)).astype(bf16)
    return probability.astype(bf16), score_grad


def leaf_visible(leaf_tree_ref, leaf_len_ref, trunk_len, seg):
    count = leaf_tree_ref.shape[0]
    in_len = jnp.sum(jnp.where(leaf_tree_ref[...] == seg, leaf_len_ref[...], 0), axis=1, keepdims=True)
    row_len = jnp.concatenate([in_len] * LEAF, axis=0)
    leaf_rows = LEAF * count
    shape = (leaf_rows, TRUNK + leaf_rows)
    row = lax.broadcasted_iota(jnp.int32, shape, 0)
    col = lax.broadcasted_iota(jnp.int32, shape, 1)
    row_pos = (row >= count).astype(jnp.int32)
    leaf_col = col - TRUNK
    col_pos = (leaf_col >= count).astype(jnp.int32)
    own = (row - row_pos * count == leaf_col - col_pos * count) & (col_pos <= row_pos)
    visible = ((col < trunk_len) & (col < TRUNK)) | ((col >= TRUNK) & own)
    return visible & (row_pos < row_len)


def weight_pairs(w_key_ref, w_value_ref, to_ref, core):
    chips, block = to_ref.shape[1:3]
    pairs = []
    for chip in range(chips):
        rows = pl.ds(pl.multiple_of((2 * chip + core) * block, block), block)
        pairs += [(w.at[rows, :], to_ref.at[part, chip]) for part, w in enumerate((w_key_ref, w_value_ref))]
    return pairs


def trunk_kernel(
    q_in, g_in, k_in, v_in, trunk_len_in, w_key_ref, w_value_ref,
    dq_ref, dkv_ref, own_ref, give_ref,
    q_ref, g_ref, k_ref, v_ref, trunk_len_ref, ds_buf, p_buf, dq_buf, dkv_buf, give_buf,
    sems, out_sems, own_sems, give_sems, gave_sems,
):
    trunk = pl.ds(0, TRUNK)
    core = lax.axis_index("kvh") & 1
    chips = own_ref.shape[1]
    loads = copies(
        [
            (trunk_len_in, trunk_len_ref),
            (k_in.at[trunk, :], k_ref),
            (v_in.at[trunk, :], v_ref),
            (q_in.at[trunk, :], q_ref),
            (g_in.at[trunk, :], g_ref),
        ],
        sems,
    )
    give_loads = copies(weight_pairs(w_key_ref, w_value_ref, give_buf, 1 - core), give_sems)
    own_loads = copies(weight_pairs(w_key_ref, w_value_ref, own_ref, core), own_sems)
    for load in loads:
        load.wait()
    trunk_len = trunk_len_ref[lax.axis_index("seg")]
    keys = k_ref[...]
    values = v_ref[...]
    row = lax.broadcasted_iota(jnp.int32, (TRUNK, TRUNK), 0)
    col = lax.broadcasted_iota(jnp.int32, (TRUNK, TRUNK), 1)
    visible = (col <= row) & (row < trunk_len)
    stores = []
    for g in range(GROUP):
        columns = slice(g * HEAD, (g + 1) * HEAD)
        rows = slice(g * TRUNK, (g + 1) * TRUNK)
        scores = dot(q_ref[:, columns], keys, (1, 1)) * SCALE
        prob_grad = dot(g_ref[:, columns], values, (1, 1))
        p_buf[rows, :], ds_buf[rows, :] = softmax_grads(scores, prob_grad, visible)
        if g == 1:
            for i, load in enumerate(give_loads):
                load.wait()
                part, chip = i % 2, i // 2
                stores += copies([(give_buf.at[part, chip], give_ref.at[part, chip])], gave_sems.at[pl.ds(i, 1)])
    query_grad = dot(ds_buf[...], keys, (1, 0)) * SCALE
    for g in range(GROUP):
        dq_buf[:, g * HEAD : (g + 1) * HEAD] = query_grad[g * TRUNK : (g + 1) * TRUNK, :].astype(bf16)
    head_q = jnp.concatenate([q_ref[:, g * HEAD : (g + 1) * HEAD] for g in range(GROUP)], axis=0)
    head_g = jnp.concatenate([g_ref[:, g * HEAD : (g + 1) * HEAD] for g in range(GROUP)], axis=0)
    dkv_buf[:, 0:HEAD] = dot(ds_buf[...], head_q, (0, 0)) * SCALE
    dkv_buf[:, HEAD:] = dot(p_buf[...], head_g, (0, 0))
    stores += copies([(dq_buf, dq_ref.at[trunk, :]), (dkv_buf, dkv_ref)], out_sems)
    for copy in stores + own_loads:
        copy.wait()


def leaf_kernel(
    in_ref, k_ref, v_ref, leaf_tree_ref, leaf_len_ref, trunk_len_in,
    out_ref, dkv_ref, rows_ref, back_ref, q_buf, g_buf, ds_buf, p_buf, out_buf, trunk_len_ref, sem, out_sems,
):
    load = pltpu.make_async_copy(trunk_len_in, trunk_len_ref, sem)
    load.start()
    count = leaf_tree_ref.shape[0]
    leaf_rows = LEAF * count
    rows_ref[...] = in_ref[...].astype(f32)

    def gather(tile):
        parts = [rows_ref[pl.ds(tile * LEAF + a, count, OUT_ROWS), :] for a in range(LEAF)]
        return jnp.concatenate(parts, axis=0).astype(bf16)

    keys = jnp.concatenate([k_ref[0:TRUNK, :], gather(2 * GROUP)], axis=0)
    values = jnp.concatenate([v_ref[0:TRUNK, :], gather(2 * GROUP + 1)], axis=0)
    seg = lax.axis_index("seg")
    load.wait()
    visible = leaf_visible(leaf_tree_ref, leaf_len_ref, trunk_len_ref[seg], seg)
    for g in range(GROUP):
        rows = slice(g * leaf_rows, (g + 1) * leaf_rows)
        head_q = gather(g)
        head_g = gather(GROUP + g)
        q_buf[rows, :] = head_q
        g_buf[rows, :] = head_g
        scores = dot(head_q, keys, (1, 1)) * SCALE
        prob_grad = dot(head_g, values, (1, 1))
        p_buf[rows, :], ds_buf[rows, :] = softmax_grads(scores, prob_grad, visible)
    query_grad = dot(ds_buf[...], keys, (1, 0)) * SCALE
    for g in range(GROUP):
        for a in range(LEAF):
            at = g * leaf_rows + a * count
            back_ref[pl.ds(g * LEAF + a, count, BACK_ROWS), :] = query_grad[at : at + count, :]
    key_grad = dot(ds_buf[...], q_buf[...], (0, 0)) * SCALE
    value_grad = dot(p_buf[...], g_buf[...], (0, 0))
    for a in range(LEAF):
        at = TRUNK + a * count
        back_ref[pl.ds(GROUP * LEAF + a, count, BACK_ROWS), :] = key_grad[at : at + count, :]
        back_ref[pl.ds((GROUP + 1) * LEAF + a, count, BACK_ROWS), :] = value_grad[at : at + count, :]
    leaf = lax.broadcasted_iota(jnp.int32, (count, count), 1)
    number = jnp.sum(jnp.where(leaf_tree_ref[...] == seg, leaf, 0), axis=1, keepdims=True).astype(f32)
    for spare in range(BACK_TILES * LEAF, BACK_ROWS):
        back_ref[pl.ds(spare, count, BACK_ROWS), :] = jnp.broadcast_to(number, (count, HEAD))
    stores = []
    for part in range(4):
        rows = pl.ds(part * (count // 4) * BACK_ROWS, count // 4 * BACK_ROWS)
        out_buf[rows, :] = back_ref[rows, :].astype(bf16)
        stores += copies([(out_buf.at[rows, :], out_ref.at[rows, :])], out_sems.at[pl.ds(part, 1)])
    dkv_ref[:, 0:HEAD] = key_grad[0:TRUNK, :]
    dkv_ref[:, HEAD:] = value_grad[0:TRUNK, :]
    for store in stores:
        store.wait()


def back_selector(rows_ref):
    count = rows_ref.shape[0] // BACK_ROWS
    number = rows_ref[pl.ds(BACK_TILES * LEAF, count, BACK_ROWS), :].astype(jnp.int32)
    col = lax.broadcasted_iota(jnp.int32, number.shape, 1)
    hits = [((number == (col >> 1)) & ((col & 1) == a)).astype(f32) for a in range(LEAF)]
    return jnp.concatenate(hits, axis=0)[:, 0 : LEAF * count].astype(bf16)


def moved_tile(rows_ref, selector, tile):
    count = rows_ref.shape[0] // BACK_ROWS
    parts = [rows_ref[pl.ds(tile * LEAF + a, count, BACK_ROWS), :] for a in range(LEAF)]
    return dot(selector, jnp.concatenate(parts, axis=0).astype(bf16), (0, 0)).astype(bf16)


def leaf_kv_kernel(in_ref, after_ref, out_ref, rows_ref):
    rows_ref[...] = in_ref[...].astype(f32)
    selector = back_selector(rows_ref)
    for part in range(2):
        out_ref[:, part * HEAD : (part + 1) * HEAD] = moved_tile(rows_ref, selector, GROUP + part)


def leaf_query_kernel(in_ref, dq_in_ref, dq_ref, token_ref, rows_ref, dq_buf, sem):
    rows_ref[...] = in_ref[...].astype(f32)
    selector = back_selector(rows_ref)
    for tile in range(GROUP):
        dq_buf[:, tile * HEAD : (tile + 1) * HEAD] = moved_tile(rows_ref, selector, tile)
    store = pltpu.make_async_copy(dq_buf, dq_ref.at[pl.ds(TRUNK, dq_buf.shape[0]), :], sem)
    store.start()
    token_ref[...] = jnp.zeros(token_ref.shape, f32)
    store.wait()


def chip_part(kv_ref, kv_other_ref, own_ref, other_ref, block):
    kv = jnp.concatenate([kv_ref[...], kv_other_ref[...]], axis=1)
    weight = jnp.concatenate([ref[part, block] for ref in (own_ref, other_ref) for part in range(2)], axis=1)
    return dot(weight, kv, (1, 1)).astype(bf16)


def trunk_part_kernel(steps, kv_ref, kv_other_ref, own_ref, other_ref, *refs):
    count = len(steps[0]) + 1
    chips = own_ref.shape[1]
    outs, token_ref, buf, sems = refs[:count], refs[count], refs[-2], refs[-1]
    kvh = lax.axis_index("kvh")
    chip, core = kvh >> 1, kvh & 1
    stores = []
    for i, (even, odd) in enumerate(zip(steps[0] + (0,), steps[1] + (0,))):
        block = lax.rem(chip + even + core * (odd - even), chips)
        part = chip_part(kv_ref, kv_other_ref, own_ref, other_ref, block)
        if i == count - 1:
            outs[i][...] = part
        else:
            buf[i] = part
            stores.append(pltpu.make_async_copy(buf.at[i], outs[i], sems.at[i]))
            stores[-1].start()
    token_ref[...] = jnp.zeros(token_ref.shape, f32)
    for store in stores:
        store.wait()


def leaf_part_kernel(kv_ref, kv_other_ref, own_ref, other_ref, after_ref, out_ref):
    for block in range(out_ref.shape[0]):
        out_ref[block] = chip_part(kv_ref, kv_other_ref, own_ref, other_ref, block)


def hidden_kernel(leaf_ref, *refs):
    trunk_refs, (out_ref, buf, sems) = refs[:-3], refs[-3:]
    columns = buf.shape[1]
    middle = columns // 256 * HEAD
    stores = []
    for i, parts in enumerate((trunk_refs, [leaf_ref.at[chip] for chip in range(leaf_ref.shape[0])])):
        rows = pl.ds(i * TRUNK, TRUNK)
        for at, width in ((0, middle), (middle, columns - middle)):
            features = pl.ds(at, width)
            total = parts[0][features, :].astype(f32)
            for part in parts[1:]:
                total += part[features, :].astype(f32)
            buf[rows, features] = total.astype(bf16).T
            pair = (buf.at[rows, features], out_ref.at[rows, features])
            stores += copies([pair], sems.at[pl.ds(len(stores), 1)])
    for store in stores:
        store.wait()


def call(kernel, outs, in_specs, out_specs, scratch=(), flops=0, moved=0, aliases={}, limit=24):
    return pl.pallas_call(
        kernel,
        out_shape=outs,
        in_specs=in_specs,
        out_specs=out_specs,
        scratch_shapes=list(scratch),
        input_output_aliases=aliases,
        compiler_params=pltpu.CompilerParams(vmem_limit_bytes=limit * 1024 * 1024),
        cost_estimate=pl.CostEstimate(flops=flops, bytes_accessed=moved, transcendentals=0),
    )


def shards(queries, key_rows, value_rows, grad_out, w_key, w_value, trunk_len, leaf_len, leaf_tree):
    count = lax.axis_size("seg")
    heads = lax.axis_size("kvh")
    chips = heads // 2
    leaf_rows = LEAF * count
    row_width = queries.shape[1]
    hidden = w_key.shape[0]
    columns = hidden // heads
    out = jax.ShapeDtypeStruct
    dma = pltpu.SemaphoreType.DMA

    vm = pltpu.VMEM

    send = call(
        send_kernel,
        out((count * OUT_ROWS, HEAD), bf16),
        [hbm] * 5,
        hbm,
        [
            vm((count, count), jnp.int32),
            vm((leaf_rows, row_width), bf16),
            vm((leaf_rows, row_width), bf16),
            vm((leaf_rows, HEAD), bf16),
            vm((leaf_rows, HEAD), bf16),
            vm((count * OUT_ROWS, HEAD), f32),
            vm((count * OUT_ROWS, HEAD), bf16),
            dma((5,)),
            dma((4,)),
        ],
        flops=10**8,
        moved=10**6,
        limit=60,
    )(queries, grad_out, key_rows, value_rows, leaf_tree)
    got = lax.all_to_all(
        send.reshape(count, OUT_ROWS, HEAD), "seg", split_axis=0, concat_axis=0, tiled=True
    ).reshape(count * OUT_ROWS, HEAD)

    keys_all = TRUNK + leaf_rows
    dq, trunk_dkv, own, give = call(
        trunk_kernel,
        [
            out(queries.shape, bf16),
            out((TRUNK, 2 * HEAD), f32),
            out((2, chips, columns, HEAD), bf16),
            out((2, chips, columns, HEAD), bf16),
        ],
        [hbm] * 7,
        [hbm] * 2 + [vmem, hbm],
        [
            vm((TRUNK, row_width), bf16),
            vm((TRUNK, row_width), bf16),
            vm((TRUNK, HEAD), bf16),
            vm((TRUNK, HEAD), bf16),
            pltpu.SMEM((count,), jnp.int32),
            vm((GROUP * TRUNK, TRUNK), bf16),
            vm((GROUP * TRUNK, TRUNK), bf16),
            vm((TRUNK, row_width), bf16),
            vm((TRUNK, 2 * HEAD), f32),
            vm((2, chips, columns, HEAD), bf16),
            dma((5,)),
            dma((2,)),
            dma((2 * chips,)),
            dma((2 * chips,)),
            dma((2 * chips,)),
        ],
        flops=4 * 10**10,
        moved=10**7,
        limit=60,
    )(queries, grad_out, key_rows, value_rows, trunk_len, w_key, w_value)

    def swap(value):
        return lax.ppermute(value, "kvh", [(i, i ^ 1) for i in range(heads)])

    other = swap(give)

    back, leaf_dkv = call(
        leaf_kernel,
        [out((count * BACK_ROWS, HEAD), bf16), out((TRUNK, 2 * HEAD), f32)],
        [vmem] * 5 + [hbm],
        [hbm, vmem],
        [
            vm((count * OUT_ROWS, HEAD), f32),
            vm((count * BACK_ROWS, HEAD), f32),
            vm((GROUP * leaf_rows, HEAD), bf16),
            vm((GROUP * leaf_rows, HEAD), bf16),
            vm((GROUP * leaf_rows, keys_all), bf16),
            vm((GROUP * leaf_rows, keys_all), bf16),
            vm((count * BACK_ROWS, HEAD), bf16),
            pltpu.SMEM((count,), jnp.int32),
            dma,
            dma((4,)),
        ],
        flops=4 * 10**10,
        moved=10**6,
    )(got, key_rows, value_rows, leaf_tree, leaf_len, trunk_len)
    trunk_kv = (trunk_dkv + leaf_dkv).astype(bf16)

    part_flops = 2 * TRUNK * 4 * HEAD * chips * columns
    part_shape = (columns, TRUNK)
    steps = ((1, 3, 2), (1, 3, 2))
    *trunk_parts, token = call(
        functools.partial(trunk_part_kernel, steps),
        [out(part_shape, bf16)] * chips + [out((8, HEAD), f32)],
        [vmem] * 4,
        [hbm] * (chips - 1) + [vmem] * 2,
        [vm((chips - 1,) + part_shape, bf16), dma((chips - 1,))],
        flops=part_flops,
        moved=4 * 10**6,
    )(trunk_kv, swap(trunk_kv), own, other)
    trunk_came = [trunk_parts[-1]]
    for i in range(chips - 1):
        route = [(2 * x + c, 2 * ((x + steps[c][i]) % chips) + c) for x in range(chips) for c in range(2)]
        trunk_came.append(lax.ppermute(trunk_parts[i], "kvh", route))
    back = lax.all_to_all(
        back.reshape(count, BACK_ROWS, HEAD), "seg", split_axis=0, concat_axis=0, tiled=True
    ).reshape(count * BACK_ROWS, HEAD)
    leaf_kv = call(
        leaf_kv_kernel,
        out((leaf_rows, 2 * HEAD), bf16),
        [vmem] * 2,
        vmem,
        [vm((count * BACK_ROWS, HEAD), f32)],
        flops=10**7,
        moved=10**6,
    )(back, token)
    grad_query, token = call(
        leaf_query_kernel,
        [out(queries.shape, bf16), out((8, HEAD), f32)],
        [vmem, hbm],
        [hbm, vmem],
        [vm((count * BACK_ROWS, HEAD), f32), vm((leaf_rows, row_width), bf16), dma],
        flops=10**8,
        moved=10**6,
        aliases={1: 0},
    )(back, dq)
    parts = call(
        leaf_part_kernel,
        out((chips, columns, leaf_rows), bf16),
        [vmem] * 5,
        vmem,
        flops=10**7,
        moved=4 * 10**6,
    )(leaf_kv, swap(leaf_kv), own, other, token)
    parts, *trunk_came = lax.optimization_barrier((parts, *trunk_came))
    came = lax.all_to_all(
        parts,
        "kvh",
        split_axis=0,
        concat_axis=0,
        tiled=True,
        axis_index_groups=[[2 * x + c for x in range(chips)] for c in range(2)],
    )
    grad_hidden = call(
        hidden_kernel,
        out((TRUNK + leaf_rows, columns), bf16),
        [vmem] * (1 + chips),
        hbm,
        [vm((TRUNK + leaf_rows, columns), bf16), dma((4,))],
        flops=10**6,
        moved=10**6,
    )(came, *trunk_came)
    return (grad_query, grad_hidden)


def solution(mesh):
    in_specs = (
        P("seg", "kvh"),
        P("seg", "kvh"),
        P("seg", "kvh"),
        P("seg", "kvh"),
        P(None, "kvh"),
        P(None, "kvh"),
        P(),
        P(),
        P(),
    )
    out_specs = (P("seg", "kvh"), P("seg", "kvh"))
    return jax.shard_map(shards, mesh=mesh, in_specs=in_specs, out_specs=out_specs, check_vma=False)
```
